256 devices in a mesh: gx: 32 (over z, y_hi, core), gy: 8 (over x, y_lo).
Axes of the slice: x: 4, y: 4 (y_hi: 2, y_lo: 2; y = y_hi * 2 + y_lo), z: 8, core: 2. Of those that a mesh axis runs over, the one named last changes fastest.
Arguments:
- positions: float32 [3, 65536], P(None, ('gx', 'gy')), may hold values from 0.3 to 63.7, as said below
- species: int32 [65536], P(('gx', 'gy')), may hold values from 0 to 9
- face_rows: int32 [4, 32768], P(None, ('gx', 'gy')), may hold values from 0 to 255, as said below
- corner_rows: int32 [4, 16384], P(None, ('gx', 'gy')), may hold values from 0 to 255, as said below
- pair_recv: int32 [13312, 128], P(('gx', 'gy')), may hold values from 0 to 255, as said below
- pair_send: int32 [13312, 128], P(('gx', 'gy')), may hold values from 0 to 1023, as said below
- block_count: int32 [256], P(('gx', 'gy')), may hold values from 0 to 52, as said below
- embedding: float32 [10, 128], replicated, may hold values from -6 to 6
- radial_in: float32 [2, 8, 64], replicated, may hold values from -2 to 2
- radial_mid: float32 [2, 64, 64], replicated, may hold values from -0.75 to 0.75
- radial_out: float32 [2, 64, 384], replicated, may hold values from -0.75 to 0.75
- self_weight: float32 [2, 128, 128], replicated, may hold values from -0.5 to 0.5
- product_weight: float32 [2, 512, 128], replicated, may hold values from -0.25 to 0.25
- readout_linear: float32 [128], replicated, may hold values from -0.5 to 0.5
- readout_hidden: float32 [128, 16], replicated, may hold values from -0.5 to 0.5
- readout_final: float32 [16], replicated, may hold values from -1.5 to 1.5
Outputs:
- forces: float32 [3, 65536], P(None, ('gx', 'gy'))
- atom_energy: float32 [65536], P(('gx', 'gy'))
The draws below stay inside these ranges and needn't reach their ends.
Inputs may be any that keep to these rules, and one draw needn't show every extreme that they name: `positions`: x and y lie inside 0 to 2, z inside 0 to 64; the two atoms of any pair are more than 0.5 apart. `face_rows`: local indices of the domain's own atoms, distinct within a row. `corner_rows`: local indices of the domain's own atoms, distinct within a row. `pair_recv`: local indices of the domain's own atoms. `pair_send`: indices into the domain's extended list of 1024 atoms, never the receiver itself. `block_count`: a multiple of 4; 52 on some domain in every draw.
All inputs are finite; a program needn't handle non-finite values.
Results may differ from the reference program's by a relative error of at most 0.0003.
Values sent between devices are 32-bit elements; how exact they have to be, the bound alone decides.
A program may use at most 128 MiB of HBM per device.

```python
import jax
import jax.numpy as jnp
import numpy as np
from jax import lax

C = 128
RH = 64
NB = 8
SPECIES = 10
RD = 16
PB = 128
GB = 4
LAT = 2
LZ = 64
ATOM_DEV = 256
FACE = 128
CORNER = 64
NBLK = 52
ATOMS = 65536
N_GX = 32
N_GY = 8


near_offsets = [[offset_code // 9 - 1, offset_code // 3 % 3 - 1, offset_code % 3 - 1] for offset_code in range(27) if offset_code != 13]


far_offsets = [[shift_x, shift_y, shift_z] for shift_z in (-3, 3) for shift_x in (-1, 0, 1) for shift_y in (-1, 0, 1)]


offset_table = np.array(near_offsets + far_offsets, dtype=np.int32)


tier_table = np.array([2] * 26 + [1] * 18, dtype=np.int32)


def lattice_layout(key):
    devices = ATOMS // ATOM_DEV
    site_keys = jax.random.split(key, devices)

    def permute_sites(site_key):
        return jax.random.permutation(site_key, ATOM_DEV)
    orders = jax.vmap(permute_sites)(site_keys).astype(jnp.int32)
    atoms_at = jnp.argsort(orders, axis=1, stable=True).astype(jnp.int32)
    return (orders, atoms_at)


def boundary_tables(key):
    orders, atoms_at = lattice_layout(key)
    devices = ATOMS // ATOM_DEV
    grid_a = jnp.arange(LAT, dtype=jnp.int32)[:, None]
    grid_z = jnp.arange(LZ, dtype=jnp.int32)[None, :]
    face_grids = [((LAT - 1) * LAT + grid_a) * LZ + grid_z, (0 * LAT + grid_a) * LZ + grid_z, (grid_a * LAT + LAT - 1) * LZ + grid_z, grid_a * LAT * LZ + grid_z]
    face_sites = jnp.stack([site_grid.reshape(-1) for site_grid in face_grids])
    line_z = jnp.arange(LZ, dtype=jnp.int32)
    corner_sites = jnp.stack([((LAT - 1) * LAT + LAT - 1) * LZ + line_z, (LAT - 1) * LAT * LZ + line_z, (LAT - 1) * LZ + line_z, line_z])
    face_table = atoms_at[:, face_sites].transpose(1, 0, 2).reshape(4, devices * FACE)
    corner_table = atoms_at[:, corner_sites].transpose(1, 0, 2).reshape(4, devices * CORNER)
    return (face_table.astype(jnp.int32), corner_table.astype(jnp.int32))


def pair_tables(key):
    orders, atoms_at = lattice_layout(key)
    choose_key = jax.random.fold_in(key, 101)
    devices = ATOMS // ATOM_DEV
    site = jnp.arange(ATOM_DEV, dtype=jnp.int32)
    coord_x = site // (LAT * LZ)
    coord_y = site // LZ % LAT
    coord_z = site % LZ
    offsets = jnp.asarray(offset_table)
    tiers = jnp.asarray(tier_table)
    near_x = coord_x[:, None] + offsets[None, :, 0]
    near_y = coord_y[:, None] + offsets[None, :, 1]
    near_z = coord_z[:, None] + offsets[None, :, 2]
    valid = (near_z >= 0) & (near_z < LZ)
    out_x = jnp.where(near_x < 0, -1, jnp.where(near_x >= LAT, 1, 0))
    out_y = jnp.where(near_y < 0, -1, jnp.where(near_y >= LAT, 1, 0))
    local_x = (near_x + LAT) % LAT
    local_y = (near_y + LAT) % LAT
    clip_z = jnp.clip(near_z, 0, LZ - 1)
    local_site = (local_x * LAT + local_y) * LZ + clip_z
    face_slot = jnp.where(out_x != 0, (out_x == 1).astype(jnp.int32), 2 + (out_y == 1).astype(jnp.int32))
    face_rank = jnp.where(out_x != 0, local_y * LZ + clip_z, local_x * LZ + clip_z)
    corner_slot = 2 * (out_x == 1).astype(jnp.int32) + (out_y == 1).astype(jnp.int32)
    ghost_face = ATOM_DEV + face_slot * FACE + face_rank
    ghost_corner = ATOM_DEV + 4 * FACE + corner_slot * CORNER + clip_z
    inside = (out_x == 0) & (out_y == 0)
    both_out = (out_x != 0) & (out_y != 0)
    candidates = ATOM_DEV * offsets.shape[0]
    ranks = (valid.astype(jnp.int32) * tiers[None, :]).reshape(-1)

    def one_domain(atoms_here, device_key):
        pick_key, shuffle_key = jax.random.split(device_key)
        sender = jnp.where(inside, atoms_here[local_site], jnp.where(both_out, ghost_corner, ghost_face)).reshape(-1)
        receiver = jnp.broadcast_to(atoms_here[:, None], near_x.shape).reshape(-1)
        scores = ranks * candidates + jax.random.permutation(pick_key, candidates).astype(jnp.int32)
        picked = jnp.argsort(-scores, stable=True)[:NBLK * PB]
        picked = picked[jax.random.permutation(shuffle_key, NBLK * PB)]
        return (receiver[picked], sender[picked])
    device_keys = jax.random.split(choose_key, devices)
    receivers, senders = jax.vmap(one_domain)(atoms_at, device_keys)
    return (receivers.reshape(devices * NBLK, PB).astype(jnp.int32), senders.reshape(devices * NBLK, PB).astype(jnp.int32))


def draw_positions(key, part):
    orders, atoms_at = lattice_layout(key)
    key = jax.random.fold_in(key, 11)
    coord_x = orders // (LAT * LZ)
    coord_y = orders // LZ % LAT
    coord_z = orders % LZ
    centre = jnp.stack([coord_x, coord_y, coord_z]).astype(jnp.float32) + 0.5
    jitter = jax.random.uniform(key, centre.shape, jnp.float32, -0.2, 0.2)
    return (centre + jitter).reshape(3, ATOMS)


def draw_face_rows(key, part):
    face_table, corner_table = boundary_tables(key)
    return face_table


def draw_corner_rows(key, part):
    face_table, corner_table = boundary_tables(key)
    return corner_table


def draw_pair_recv(key, part):
    receivers, senders = pair_tables(key)
    return receivers


def draw_pair_send(key, part):
    receivers, senders = pair_tables(key)
    return senders


def draw_block_count(key, part):
    key = jax.random.fold_in(key, 31)
    devices = ATOMS // ATOM_DEV
    heavy_key, light_key, chosen_key = jax.random.split(key, 3)
    heavy = jax.random.randint(heavy_key, (devices,), 0, 4) == 0
    light = GB * (NBLK // (4 * GB) + jax.random.randint(light_key, (devices,), 0, 3))
    light = jnp.minimum(light, NBLK)
    counts = jnp.where(heavy, NBLK, light)
    chosen = jax.random.randint(chosen_key, (), 0, devices)
    counts = jnp.where(jnp.arange(devices) == chosen, NBLK, counts)
    return counts.astype(jnp.int32)


def touch_ends(values, key, least, high):
    index_at = [jax.random.randint(jax.random.fold_in(key, axis), (), 0, length) for axis, length in enumerate(values.shape)]
    main_axis = values.shape.index(max(values.shape))
    neighbour = index_at[:main_axis] + [(index_at[main_axis] + 1) % values.shape[main_axis]] + index_at[main_axis + 1:]
    return values.at[tuple(index_at)].set(least).at[tuple(neighbour)].set(high)


def bell_draw(stream_key, dims, deviation, most, kind=jnp.bfloat16):
    drawn = jax.random.normal(stream_key, dims, jnp.float32) * deviation
    return jnp.minimum(jnp.maximum(drawn, -most), most).astype(kind)


def setup_inputs(seed: int = 0) -> dict:
    splits = jax.random.split(jax.random.key(seed), 17)
    return {
        "positions": draw_positions(jax.random.fold_in(splits[16], 71), 0),
        "species": touch_ends(jax.random.randint(splits[1], (ATOMS,), 0, SPECIES), jax.random.fold_in(splits[1], 1), 0, SPECIES - 1).astype(jnp.int32),
        "face_rows": draw_face_rows(jax.random.fold_in(splits[16], 71), 0),
        "corner_rows": draw_corner_rows(jax.random.fold_in(splits[16], 71), 0),
        "pair_recv": draw_pair_recv(jax.random.fold_in(splits[16], 71), 0),
        "pair_send": draw_pair_send(jax.random.fold_in(splits[16], 71), 0),
        "block_count": draw_block_count(jax.random.fold_in(splits[16], 71), 0),
        "embedding": bell_draw(splits[7], (SPECIES, C), 1.0, 6.0, jnp.float32),
        "radial_in": bell_draw(splits[8], (2, NB, RH), NB ** -0.5, 2.0, jnp.float32),
        "radial_mid": bell_draw(splits[9], (2, RH, RH), RH ** -0.5, 0.75, jnp.float32),
        "radial_out": bell_draw(splits[10], (2, RH, 3 * C), RH ** -0.5, 0.75, jnp.float32),
        "self_weight": bell_draw(splits[11], (2, C, C), C ** -0.5, 0.5, jnp.float32),
        "product_weight": bell_draw(splits[12], (2, 4 * C, C), (4 * C) ** -0.5, 0.25, jnp.float32),
        "readout_linear": bell_draw(splits[13], (C,), C ** -0.5, 0.5, jnp.float32),
        "readout_hidden": bell_draw(splits[14], (C, RD), C ** -0.5, 0.5, jnp.float32),
        "readout_final": bell_draw(splits[15], (RD,), RD ** -0.5, 1.5, jnp.float32),
    }


highest = lax.Precision.HIGHEST
inv_neigh = 0.25
cutoff = 2.5
sharpness = 2.0
root_three = 3.0 ** 0.5
root_five = 5.0 ** 0.5
root_fifteen = 15.0 ** 0.5
face_steps = ((1, 0), (-1, 0), (0, 1), (0, -1))
corner_steps = ((1, 1), (1, -1), (-1, 1), (-1, -1))

def harmonics(unit_vec):
    coord_x = unit_vec[0]
    coord_y = unit_vec[1]
    coord_z = unit_vec[2]
    return jnp.stack([jnp.ones_like(coord_x), root_three * coord_x, root_three * coord_y, root_three * coord_z, root_fifteen * coord_x * coord_y, root_fifteen * coord_y * coord_z, 0.5 * root_five * (3.0 * coord_z * coord_z - 1.0), root_fifteen * coord_x * coord_z, 0.5 * root_fifteen * (coord_x * coord_x - coord_y * coord_y)])

def pair_messages(vectors, sender_feats, radial_in, radial_mid, radial_out):
    distance = jnp.sqrt(lax.optimization_barrier(jnp.sum(vectors * vectors, axis=0)))
    harmonic_vals = harmonics(vectors / distance[None, :])
    scaled_dist = distance / cutoff
    envelope = jnp.where(scaled_dist < 1.0, (1.0 - scaled_dist * scaled_dist) ** 2, 0.0)
    basis_count = radial_in.shape[0]
    centres = jnp.arange(basis_count, dtype=jnp.float32) * (cutoff / (basis_count - 1))
    radial_basis = jnp.exp(-sharpness * (distance[None, :] - centres[:, None]) ** 2) * envelope[None, :]
    hidden_one = jax.nn.silu(jnp.einsum('bp,bh->ph', radial_basis, radial_in, precision=highest))
    hidden_two = jax.nn.silu(jnp.dot(hidden_one, radial_mid, precision=highest))
    radial = jnp.dot(hidden_two, radial_out, precision=highest)
    pair_total = radial.shape[0]
    channels = sender_feats.shape[1]
    radial = radial.reshape(pair_total, 3, channels)
    expanded = jnp.concatenate([radial[:, 0:1, :], jnp.broadcast_to(radial[:, 1:2, :], (pair_total, 3, channels)), jnp.broadcast_to(radial[:, 2:3, :], (pair_total, 5, channels))], axis=1)
    return expanded * jnp.transpose(harmonic_vals)[:, :, None] * sender_feats[:, None, :]

def node_update(accum, previous, self_weight, product_weight):
    scalar_part = accum[..., 0, :]
    vector_norm = lax.optimization_barrier(jnp.sum(accum[..., 1:4, :] * accum[..., 1:4, :], axis=-2))
    tensor_norm = lax.optimization_barrier(jnp.sum(accum[..., 4:9, :] * accum[..., 4:9, :], axis=-2))
    invariants = jnp.concatenate([scalar_part, vector_norm, tensor_norm, scalar_part * scalar_part], axis=-1)
    return jnp.dot(previous, self_weight, precision=highest) + jnp.dot(invariants, product_weight, precision=highest)

def atom_energies(first_feats, second_feats, readout_linear, readout_hidden, readout_final):
    hidden = jax.nn.silu(jnp.dot(second_feats, readout_hidden, precision=highest))
    return jnp.dot(first_feats, readout_linear, precision=highest) + jnp.dot(hidden, readout_final, precision=highest)

def extend_rows(values, face_table, corner_table):
    pieces = [values]
    for slot_index in range(4):
        outgoing = jnp.take_along_axis(values, face_table[:, :, slot_index, :, None], axis=2)
        pieces.append(jnp.roll(outgoing, face_steps[slot_index], axis=(0, 1)))
    for slot_index in range(4):
        outgoing = jnp.take_along_axis(values, corner_table[:, :, slot_index, :, None], axis=2)
        pieces.append(jnp.roll(outgoing, corner_steps[slot_index], axis=(0, 1)))
    return jnp.concatenate(pieces, axis=2)

def ghost_shift(face_count, corner_count):
    blocks = []
    for step_x, step_y in face_steps:
        blocks.append(jnp.broadcast_to(jnp.array([-step_x * LAT, -step_y * LAT, 0.0], dtype=jnp.float32), (face_count, 3)))
    for step_x, step_y in corner_steps:
        blocks.append(jnp.broadcast_to(jnp.array([-step_x * LAT, -step_y * LAT, 0.0], dtype=jnp.float32), (corner_count, 3)))
    return jnp.concatenate(blocks, axis=0)

def reference(positions, species, face_rows, corner_rows, pair_recv, pair_send, block_count, embedding, radial_in, radial_mid, radial_out, self_weight, product_weight, readout_linear, readout_hidden, readout_final):
    devices = N_GX * N_GY
    face_table = face_rows.reshape(4, N_GX, N_GY, FACE).transpose(1, 2, 0, 3)
    corner_table = corner_rows.reshape(4, N_GX, N_GY, CORNER).transpose(1, 2, 0, 3)
    onehot = (species.reshape(N_GX, N_GY, ATOM_DEV)[..., None] == jnp.arange(SPECIES, dtype=jnp.int32)).astype(jnp.float32)
    embedded = jnp.einsum('abns,sc->abnc', onehot, embedding, precision=highest)
    channels = embedding.shape[1]
    zero_ext = extend_rows(embedded, face_table, corner_table).reshape(devices, -1, channels)
    receivers = pair_recv.reshape(devices, NBLK * PB)
    senders = pair_send.reshape(devices, NBLK * PB)
    counts = block_count.reshape(devices)
    offsets = ghost_shift(FACE, CORNER)

    def run_layer(layer_index, pos_flat, feat_ext, previous):

        def one_domain(inputs):
            pos_one, feat_one, recv_one, send_one, count_one, prev_one = inputs
            vectors = jnp.transpose(pos_one[send_one] - pos_one[recv_one])
            messages = pair_messages(vectors, feat_one[send_one], radial_in[layer_index], radial_mid[layer_index], radial_out[layer_index])
            live = (jnp.arange(recv_one.shape[0]) < count_one * PB).astype(jnp.float32)
            flat = messages.reshape(recv_one.shape[0], -1) * live[:, None]
            accum = jax.ops.segment_sum(flat, recv_one, num_segments=ATOM_DEV) * inv_neigh
            return node_update(accum.reshape(ATOM_DEV, 9, channels), prev_one, self_weight[layer_index], product_weight[layer_index])
        saved = jax.checkpoint(one_domain)
        return lax.map(saved, (pos_flat, feat_ext, receivers, senders, counts, previous))

    def total_energy(pos_rows):
        pos_ext = extend_rows(pos_rows, face_table, corner_table)
        pos_ext = pos_ext.at[:, :, ATOM_DEV:, :].add(offsets)
        pos_flat = pos_ext.reshape(devices, -1, 3)
        first_feats = run_layer(0, pos_flat, zero_ext, embedded.reshape(devices, ATOM_DEV, channels))
        first_ext = extend_rows(first_feats.reshape(N_GX, N_GY, ATOM_DEV, channels), face_table, corner_table).reshape(devices, -1, channels)
        second_feats = run_layer(1, pos_flat, first_ext, first_feats)
        energies = atom_energies(first_feats, second_feats, readout_linear, readout_hidden, readout_final)
        return (jnp.sum(energies), energies)
    pos_rows = positions.reshape(3, N_GX, N_GY, ATOM_DEV).transpose(1, 2, 3, 0)
    gradient, energies = jax.grad(total_energy, has_aux=True)(pos_rows)
    forces = -jnp.transpose(gradient, (3, 0, 1, 2)).reshape(3, ATOMS)
    return (forces, energies.reshape(ATOMS))
```

```python
from functools import partial

import jax
import jax.numpy as jnp
from jax import lax
from jax.experimental import pallas as pl
from jax.experimental.pallas import tpu as pltpu
from jax.sharding import PartitionSpec as P

f32 = jnp.float32
bf16 = jnp.bfloat16
i32 = jnp.int32

LAT = 2
C = 128
RH = 64
NB = 8
ATOMS = 256
EXT = 1024
NBLK = 52
PB = 128
PAIRS = NBLK * PB
TM = 512
T = 256
SUB = 128
ROWS = 56
STEPS = ((1, 0), (-1, 0), (0, 1), (0, -1), (1, 1), (1, -1), (-1, 1), (-1, -1))
CUTOFF = 2.5
SHARP = 2.0
Q3 = 3.0**0.5
Q5 = 5.0**0.5
Q15 = 15.0**0.5
INV_NEIGH = 0.25
HIGH = lax.Precision.HIGHEST
MESH = pl.DeviceIdType.MESH
L_OF_M = (0, 1, 1, 1, 2, 2, 2, 2, 2)


def dot(a, b):
    return lax.dot_general(a, b, (((1,), (0,)), ((), ())), preferred_element_type=f32)


def dot_nt(a, b):
    return lax.dot_general(a, b, (((1,), (1,)), ((), ())), preferred_element_type=f32)


def dot_exact(a, b):
    return lax.dot_general(
        a, b, (((1,), (0,)), ((), ())), precision=HIGH, preferred_element_type=f32
    )


def parts2(x):
    hi = x.astype(bf16).astype(f32)
    return hi, (x - hi).astype(bf16).astype(f32)


def parts3(x):
    hi = x.astype(bf16).astype(f32)
    rest = x - hi
    mid = rest.astype(bf16).astype(f32)
    return hi, mid, (rest - mid).astype(bf16).astype(f32)


def split2(x):
    hi = x.astype(bf16)
    return hi, (x - hi.astype(f32)).astype(bf16)


def activations(x):
    hi, lo = split2(x)
    return jnp.concatenate([hi, lo, hi, lo], axis=0)


def weights(w):
    hi, lo = parts2(w)
    return jnp.concatenate([hi, hi, lo, lo], axis=0).T.astype(bf16)


def slot_of(k):
    return (128 * k, 128) if k < 4 else (512 + 64 * (k - 4), 64)


def tile_of(k):
    return k if k < 4 else 4 + (k - 4) // 2


def kernel_body(
    sizes,
    pos,
    species,
    face_rows,
    corner_rows,
    pair_recv,
    pair_send,
    block_count,
    embedding,
    radial_in,
    radial_mid,
    radial_out,
    self_weight,
    product_weight,
    readout_linear,
    readout_hidden,
    readout_final,
    forces,
    energies,
    *scratch,
):
    (
        rows6,
        oh6,
        oh6t,
        psrc,
        posout,
        posin,
        ptab,
        geop,
        georow,
        sendrow,
        recvm,
        ohs,
        ohr,
        emb3,
        win4,
        wmid4,
        wout4,
        bmid4,
        bin4,
        bout2,
        bout1,
        z1s,
        z2s,
        rs,
        fg,
        msg,
        acc,
        acc1,
        acc2,
        gacc,
        gbuf,
        gf,
        gr,
        ge,
        f0t,
        f1t,
        fsend,
        fghost,
        fext,
        gfirst,
        gsend,
        gret,
        gv,
        fs,
        fr,
        gpout,
        gpin,
        send_sem,
        recv_sem,
    ) = scratch
    sums = (acc1, acc2)
    nx, ny = sizes
    alone = nx * ny == 1
    mx = lax.axis_index("gx")
    my = lax.axis_index("gy")

    def neighbour(k, sign):
        dx, dy = STEPS[k]
        return (lax.rem(mx + sign * dx + nx, nx), lax.rem(my + sign * dy + ny, ny))

    if not alone:
        barrier = pltpu.get_barrier_semaphore()
        for k in range(8):
            pl.semaphore_signal(barrier, inc=1, device_id=neighbour(k, 1), device_id_type=MESH)

    def copies(phase, source, target, sign):
        made = []
        for k in range(8):
            if alone:
                made.append(
                    pltpu.make_async_copy(source(k), target(k), recv_sem.at[phase * 8 + k])
                )
            else:
                made.append(
                    pltpu.make_async_remote_copy(
                        src_ref=source(k),
                        dst_ref=target(k),
                        send_sem=send_sem.at[phase * 8 + k],
                        recv_sem=recv_sem.at[phase * 8 + k],
                        device_id=neighbour(k, sign),
                        device_id_type=MESH,
                    )
                )
        return made

    def start(made):
        for c in made:
            c.start()

    def finish(made):
        for c in made:
            c.wait()

    rows6[...] = jnp.zeros_like(rows6)
    rows6[0:4, :] = face_rows[...]
    rows6[4:5, :] = jnp.concatenate([corner_rows[0:1, :], corner_rows[1:2, :]], axis=1)
    rows6[5:6, :] = jnp.concatenate([corner_rows[2:3, :], corner_rows[3:4, :]], axis=1)
    rows_t = rows6[...].astype(f32).T
    atom_sub = lax.broadcasted_iota(i32, (ATOMS, 128), 0)
    atom_lane = lax.broadcasted_iota(i32, (128, ATOMS), 1)
    for h in range(6):
        oh6[:, h * 128 : (h + 1) * 128] = (atom_sub == rows6[h : h + 1, :]).astype(bf16)
        col = jnp.broadcast_to(rows_t[:, h : h + 1], (128, ATOMS)).astype(i32)
        oh6t[h * 128 : (h + 1) * 128, :] = (atom_lane == col).astype(bf16)

    psrc[...] = jnp.zeros_like(psrc)
    psrc[0:3, :] = pos[...]
    psrc[3:4, :] = species[...].astype(f32)
    own = psrc[...]
    three = jnp.concatenate(parts3(own), axis=0).astype(bf16)
    lent = dot(three, oh6[...])
    lent = lent[0:8] + lent[8:16] + lent[16:24]
    for h in range(6):
        posout[h] = lent[:, h * 128 : (h + 1) * 128]
    if not alone:
        pl.semaphore_wait(barrier, 8)
    sent = copies(0, lambda k: posout.at[tile_of(k)], lambda k: posin.at[k], 1)
    start(sent)

    ext_sub = lax.broadcasted_iota(i32, (EXT, PB), 0)
    live = lax.broadcasted_iota(i32, (NBLK, PB), 0) < block_count[0]
    recvm[...] = jnp.where(live, pair_recv[...], -1)

    def build(b, carry):
        cols = pl.ds(pl.multiple_of(b * PB, PB), PB)
        send = pair_send[pl.ds(b, 1), :]
        ohs[:, cols] = (ext_sub == send).astype(bf16)
        ohr[:, cols] = (atom_sub == recvm[pl.ds(b, 1), :]).astype(bf16)
        sendrow[0:1, cols] = send
        return carry

    lax.fori_loop(0, NBLK, build, 0)

    emb = embedding[...]
    padding = jnp.zeros((6, C), f32)
    pieces = []
    for piece in parts3(emb):
        pieces += [piece, padding]
    pieces.append(jnp.zeros((80, C), f32))
    emb3[...] = jnp.concatenate(pieces, axis=0).T.astype(bf16)

    def prepare(t):
        win = radial_in[t]
        wmid = radial_mid[t]
        wout = radial_out[t]
        win4[...] = weights(win)
        wmid4[...] = weights(wmid)
        wout4[...] = weights(wout)

    def prepare_back(t):
        win = radial_in[t]
        wmid = radial_mid[t]
        wout = radial_out[t]
        bmid4[...] = weights(wmid.T)
        bin4[...] = jnp.concatenate([weights(win.T), jnp.zeros((8, 4 * RH), bf16)], axis=0)
        hi, lo = split2(wout)
        bout2[0:RH, :] = hi
        bout2[RH : 2 * RH, :] = lo
        bout1[...] = hi

    prepare(0)
    species16 = lax.broadcasted_iota(i32, (128, T), 0) & 15
    f0t[...] = dot(emb3[...], (species16 == species[...]).astype(bf16))

    finish(sent)

    low_half = lax.broadcasted_iota(i32, (8, 128), 1) < 64
    tiles = [own[:, 0:128], own[:, 128:256]]
    shifted = []
    for k in range(8):
        dx, dy = STEPS[k]
        got = posin[k]
        sub = lax.broadcasted_iota(i32, (8, 128), 0)
        shift = jnp.where(sub == 0, f32(dx * LAT), jnp.where(sub == 1, f32(dy * LAT), f32(0)))
        shifted.append(got - shift)
    tiles += shifted[0:4]
    tiles.append(jnp.where(low_half, shifted[4], shifted[5]))
    tiles.append(jnp.where(low_half, shifted[6], shifted[7]))
    for h in range(8):
        ptab[h] = tiles[h]

    send = pair_send[...]
    send_lo = send & 127
    send_hi = lax.shift_right_logical(send, 7)
    recv = pair_recv[...]
    recv_lo = recv & 127
    recv_hi = lax.shift_right_logical(recv, 7)

    def gather(c, lo, hi, count):
        total = jnp.zeros((NBLK, PB), f32)
        for h in range(count):
            row = jnp.broadcast_to(ptab[h][c : c + 1, :], (NBLK, PB))
            total = jnp.where(hi == h, jnp.take_along_axis(row, lo, axis=1), total)
        return total

    vec = [gather(c, send_lo, send_hi, 8) - gather(c, recv_lo, recv_hi, 2) for c in range(3)]
    sender_species = gather(3, send_lo, send_hi, 8)
    square = vec[0] * vec[0] + vec[1] * vec[1] + vec[2] * vec[2]
    square = jnp.where(live, square, 1.0)
    dist = jnp.sqrt(square)
    inv = 1.0 / dist
    ux, uy, uz = [v / dist for v in vec]
    scaled = dist * (1.0 / CUTOFF)
    inside = scaled < 1.0
    room = 1.0 - scaled * scaled
    env = jnp.where(inside, room * room, 0.0)
    denv = jnp.where(inside, (-4.0 / CUTOFF) * scaled * room, 0.0)
    values = [
        dist,
        ux,
        uy,
        uz,
        inv,
        env,
        denv,
        sender_species,
        Q3 * ux,
        Q3 * uy,
        Q3 * uz,
        Q15 * ux * uy,
        Q15 * uy * uz,
        0.5 * Q5 * (3.0 * uz * uz - 1.0),
        Q15 * ux * uz,
        0.5 * Q15 * (ux * ux - uy * uy),
    ]
    for n in range(16):
        geop[n * ROWS : n * ROWS + NBLK, :] = values[n]
    for b in range(NBLK):
        georow[:, b * PB : (b + 1) * PB] = geop[pl.ds(b, 16, stride=ROWS), :]

    def basis_of(geo, width):
        dist = geo[0:1]
        centre = lax.broadcasted_iota(i32, (NB, width), 0).astype(f32) * (CUTOFF / (NB - 1))
        away = dist - centre
        return away, jnp.exp(-SHARP * away * away)

    def radial_pass(i, carry):
        cols = pl.ds(pl.multiple_of(i * TM, TM), TM)
        geo = georow[:, cols]
        away, bump = basis_of(geo, TM)
        hi, lo = parts2(bump * geo[5:6])
        z1 = dot(win4[...], jnp.concatenate([hi, lo, hi, lo], axis=0).astype(bf16))
        z1s[:, cols] = z1
        z2 = dot(wmid4[...], activations(z1 * jax.nn.sigmoid(z1)))
        z2s[:, cols] = z2
        rs[:, cols] = dot(wout4[...], activations(z2 * jax.nn.sigmoid(z2)))
        return carry

    def radial_all():
        lax.fori_loop(0, PAIRS // TM, radial_pass, 0)

    def first_senders(cols):
        return dot(emb3[...], (species16 == georow[7:8, cols].astype(i32)).astype(bf16))

    def second_senders(cols):
        both = dot(fext[...], ohs[:, cols])
        return both[0:C] + both[C : 2 * C]

    def forward(t, senders):
        acc[...] = jnp.zeros_like(acc)

        def step(i, carry):
            base = pl.multiple_of(i * T, T)
            cols = pl.ds(base, T)
            fg[:, cols] = senders(cols)
            for s in range(0, T, SUB):
                sub = pl.ds(pl.multiple_of(base + s, SUB), SUB)
                ys = [jnp.broadcast_to(georow[8 + m : 9 + m, sub], (16, SUB)) for m in range(8)]
                for c in range(0, C, 16):
                    f = fg[c : c + 16, sub]
                    p = [rs[l * C + c : l * C + c + 16, sub] * f for l in range(3)]
                    for m in range(9):
                        value = p[0] if m == 0 else p[L_OF_M[m]] * ys[m - 1]
                        hi, lo = split2(value)
                        msg[m * C + c : m * C + c + 16, s : s + SUB] = hi
                        msg[m * C + c : m * C + c + 16, T + s : T + s + SUB] = lo
            hot = ohr[:, cols]
            acc[...] += dot_nt(msg[...], jnp.concatenate([hot, hot], axis=1))
            return carry

        lax.fori_loop(0, PAIRS // T, step, 0)
        sums[t][...] = acc[...] * INV_NEIGH

    def invariants(t):
        accn = sums[t]
        a0 = accn[0:C]
        v = accn[C : 2 * C] ** 2
        for m in range(2, 4):
            v = v + accn[m * C : (m + 1) * C] ** 2
        w = accn[4 * C : 5 * C] ** 2
        for m in range(5, 9):
            w = w + accn[m * C : (m + 1) * C] ** 2
        return jnp.concatenate([a0, v, w, a0 * a0], axis=0)

    def node(t, previous):
        return dot_exact(self_weight[t].T, previous) + dot_exact(
            product_weight[t].T, invariants(t)
        )

    def node_back(t, grad):
        accn = sums[t]
        ginv = dot_exact(product_weight[t], grad) * INV_NEIGH
        for m in range(9):
            a = accn[m * C : (m + 1) * C]
            if m == 0:
                g = ginv[0:C] + 2.0 * a * ginv[3 * C : 4 * C]
            else:
                l = L_OF_M[m]
                g = 2.0 * a * ginv[l * C : (l + 1) * C]
            hi, lo = split2(g)
            gacc[m * C : (m + 1) * C, 0:ATOMS] = hi
            gacc[m * C : (m + 1) * C, ATOMS : 2 * ATOMS] = lo

    def backward(first):
        def step(i, carry):
            base = pl.multiple_of(i * T, T)
            cols = pl.ds(base, T)
            hot = ohr[:, cols]
            gbuf[...] = dot(gacc[...], jnp.concatenate([hot, hot], axis=0))
            gys = []
            for s in range(0, T, SUB):
                sub = pl.ds(pl.multiple_of(base + s, SUB), SUB)
                ys = [jnp.broadcast_to(georow[8 + m : 9 + m, sub], (16, SUB)) for m in range(8)]
                dy = [jnp.zeros((16, SUB), f32) for m in range(8)]
                for c in range(0, C, 16):
                    f = fg[c : c + 16, sub]
                    r = [rs[l * C + c : l * C + c + 16, sub] for l in range(3)]
                    p = [x * f for x in r]
                    tot = [None, None, None]
                    for m in range(9):
                        g = gbuf[m * C + c : m * C + c + 16, s : s + SUB]
                        l = L_OF_M[m]
                        term = g if m == 0 else g * ys[m - 1]
                        tot[l] = term if tot[l] is None else tot[l] + term
                        if m > 0:
                            dy[m - 1] = dy[m - 1] + p[l] * g
                    if not first:
                        gfv = r[0] * tot[0] + r[1] * tot[1] + r[2] * tot[2]
                        hi, lo = split2(gfv)
                        gf[c : c + 16, s : s + SUB] = hi
                        gf[C + c : C + c + 16, s : s + SUB] = lo
                    for l in range(3):
                        hi, lo = split2(tot[l] * f)
                        gr[l * C + c : l * C + c + 16, s : s + SUB] = hi
                        gr[l * C + c : l * C + c + 16, T + s : T + s + SUB] = lo
                gys.append([jnp.sum(x, axis=0, keepdims=True) for x in dy])
            gy = [jnp.concatenate([part[m] for part in gys], axis=1) for m in range(8)]
            if not first:
                ge[...] += dot_nt(ohs[:, cols], gf[...])
            both = dot(bout2[...], gr[:, 0:T])
            gh2 = both[0:RH] + both[RH : 2 * RH] + dot(bout1[...], gr[:, T : 2 * T])
            z2 = z2s[:, cols]
            sg = jax.nn.sigmoid(z2)
            gh1 = dot(bmid4[...], activations(gh2 * (sg * (1.0 + z2 * (1.0 - sg)))))
            z1 = z1s[:, cols]
            sg = jax.nn.sigmoid(z1)
            gb = dot(bin4[...], activations(gh1 * (sg * (1.0 + z1 * (1.0 - sg)))))[0:NB]
            geo = georow[:, cols]
            away, bump = basis_of(geo, T)
            slope = bump * (geo[6:7] - (2.0 * SHARP) * away * geo[5:6])
            gdist = jnp.sum(gb * slope, axis=0, keepdims=True)
            ux, uy, uz = geo[1:2], geo[2:3], geo[3:4]
            gux = Q3 * gy[0] + Q15 * (uy * gy[3] + uz * gy[6] + ux * gy[7])
            guy = Q3 * gy[1] + Q15 * (ux * gy[3] + uz * gy[4] - uy * gy[7])
            guz = Q3 * gy[2] + Q15 * (uy * gy[4] + ux * gy[6]) + (3.0 * Q5) * uz * gy[5]
            along = gux * ux + guy * uy + guz * uz
            inv = geo[4:5]
            pull = gdist - inv * along
            out = [pull * ux + inv * gux, pull * uy + inv * guy, pull * uz + inv * guz]
            if not first:
                for n in range(3):
                    gv[n : n + 1, cols] = out[n]
            else:
                out = [out[n] + gv[n : n + 1, cols] for n in range(3)]
                cut = [parts2(x) for x in out]
                zero = jnp.zeros((2, T), f32)
                base8 = jnp.concatenate([x[0] for x in cut] + [x[1] for x in cut] + [zero], axis=0)
                idx = sendrow[0:1, cols]
                high = lax.shift_right_logical(idx, 7)
                lhs = jnp.concatenate(
                    [jnp.where(high == h, base8, 0.0) for h in range(8)], axis=0
                ).astype(bf16)
                low = (lax.broadcasted_iota(i32, (128, T), 0) == (idx & 127)).astype(bf16)
                fs[...] += dot_nt(lhs, low)
                lhs = jnp.concatenate([base8, jnp.zeros((8, T), f32)], axis=0).astype(bf16)
                fr[...] += dot_nt(lhs, hot)
            return carry

        lax.fori_loop(0, PAIRS // T, step, 0)

    radial_all()
    forward(0, first_senders)
    f1t[...] = node(0, f0t[...])

    feat = f1t[...]
    rows = feat.T
    gathered = dot(oh6t[...], jnp.concatenate(parts3(rows), axis=1).astype(bf16))
    fsend[...] = gathered[:, 0:C] + gathered[:, C : 2 * C] + gathered[:, 2 * C : 3 * C]
    sent = copies(
        1, lambda k: fsend.at[pl.ds(*slot_of(k))], lambda k: fghost.at[pl.ds(*slot_of(k))], 1
    )
    start(sent)
    gsend[0:ATOMS, :] = jnp.zeros((ATOMS, C), f32)
    prepare(1)
    prepare_back(1)
    radial_all()
    finish(sent)
    hi, lo = split2(feat)
    fext[0:C, 0:ATOMS] = hi
    fext[C : 2 * C, 0:ATOMS] = lo
    hi, lo = split2(fghost[...].T)
    fext[0:C, ATOMS:EXT] = hi
    fext[C : 2 * C, ATOMS:EXT] = lo

    forward(1, second_senders)
    second = node(1, feat)
    hidden = dot_exact(readout_hidden[...].T, second)
    sg = jax.nn.sigmoid(hidden)
    energies[...] = dot_exact(readout_linear[...], feat) + dot_exact(
        readout_final[...], hidden * sg
    )
    weight = readout_final[...].T
    ghidden = weight * (sg * (1.0 + hidden * (1.0 - sg)))
    gsecond = dot_exact(readout_hidden[...], ghidden)
    gfirst[...] = readout_linear[...].T + dot_exact(self_weight[1], gsecond)
    node_back(1, gsecond)
    ge[...] = jnp.zeros_like(ge)
    backward(False)

    gsend[...] = ge[:, 0:C] + ge[:, C : 2 * C]

    def ghost(k):
        offset, size = slot_of(k)
        return gsend.at[pl.ds(ATOMS + offset, size)]

    sent = copies(2, ghost, lambda k: gret.at[pl.ds(*slot_of(k))], -1)
    start(sent)
    prepare(0)
    prepare_back(0)
    radial_all()

    def senders_pass(i, carry):
        cols = pl.ds(pl.multiple_of(i * T, T), T)
        fg[:, cols] = first_senders(cols)
        return carry

    lax.fori_loop(0, PAIRS // T, senders_pass, 0)
    fs[...] = jnp.zeros_like(fs)
    fr[...] = jnp.zeros_like(fr)
    finish(sent)
    returned = dot(oh6[...], jnp.concatenate(parts3(gret[...]), axis=1).astype(bf16))
    mine = gsend[0:ATOMS, :] + returned[:, 0:C] + returned[:, C : 2 * C] + returned[:, 2 * C :]
    node_back(0, gfirst[...] + mine.T)
    backward(True)

    nothing = jnp.zeros((5, 128), f32)
    tiles = []
    for h in range(8):
        part = fs[8 * h : 8 * h + 8, :]
        tiles.append(jnp.concatenate([part[0:3] + part[3:6], nothing], axis=0))
    for h in range(6):
        gpout[h] = tiles[h + 2]
    sent = copies(3, lambda k: gpout.at[tile_of(k)], lambda k: gpin.at[k], -1)
    start(sent)
    own = jnp.concatenate(tiles[0:2], axis=1)[0:3] - (fr[0:3, :] + fr[3:6, :])
    finish(sent)
    back = [gpin[k] for k in range(4)]
    back.append(jnp.where(low_half, gpin[4], gpin[5]))
    back.append(jnp.where(low_half, gpin[6], gpin[7]))
    three = jnp.concatenate(parts3(jnp.concatenate(back, axis=1)), axis=0).astype(bf16)
    added = dot_nt(three, oh6[...])
    forces[...] = -(own + added[0:3] + added[8:11] + added[16:19])


SCRATCH = (
    ((8, 128), i32),
    ((ATOMS, 768), bf16),
    ((768, ATOMS), bf16),
    ((8, ATOMS), f32),
    ((6, 8, 128), f32),
    ((8, 8, 128), f32),
    ((8, 8, 128), f32),
    ((16 * ROWS, 128), f32),
    ((16, PAIRS), f32),
    ((8, PAIRS), i32),
    ((NBLK, PB), i32),
    ((EXT, PAIRS), bf16),
    ((ATOMS, PAIRS), bf16),
    ((C, 128), bf16),
    ((RH, 4 * NB), bf16),
    ((RH, 4 * RH), bf16),
    ((3 * C, 4 * RH), bf16),
    ((RH, 4 * RH), bf16),
    ((2 * NB, 4 * RH), bf16),
    ((2 * RH, 3 * C), bf16),
    ((RH, 3 * C), bf16),
    ((RH, PAIRS), f32),
    ((RH, PAIRS), f32),
    ((3 * C, PAIRS), f32),
    ((C, PAIRS), f32),
    ((9 * C, 2 * T), bf16),
    ((9 * C, ATOMS), f32),
    ((9 * C, ATOMS), f32),
    ((9 * C, ATOMS), f32),
    ((9 * C, 2 * ATOMS), bf16),
    ((9 * C, T), f32),
    ((2 * C, T), bf16),
    ((3 * C, 2 * T), bf16),
    ((EXT, 2 * C), f32),
    ((C, ATOMS), f32),
    ((C, ATOMS), f32),
    ((768, C), f32),
    ((768, C), f32),
    ((2 * C, EXT), bf16),
    ((C, ATOMS), f32),
    ((EXT, C), f32),
    ((768, C), f32),
    ((8, PAIRS), f32),
    ((64, 128), f32),
    ((16, ATOMS), f32),
    ((6, 8, 128), f32),
    ((8, 8, 128), f32),
)


def solution(mesh):
    sizes = (mesh.shape["gx"], mesh.shape["gy"])

    def per_device(positions, species, face_rows, corner_rows, pair_recv, pair_send, *rest):
        block_count = rest[0]
        params = list(rest[1:])
        params[6] = params[6].reshape(1, -1)
        params[8] = params[8].reshape(1, -1)
        vmem = pl.BlockSpec(memory_space=pltpu.VMEM)
        smem = pl.BlockSpec(memory_space=pltpu.SMEM)
        remote = {"collective_id": 0} if sizes != (1, 1) else {}
        forces, energies = pl.pallas_call(
            partial(kernel_body, sizes),
            out_shape=[
                jax.ShapeDtypeStruct((3, ATOMS), f32),
                jax.ShapeDtypeStruct((1, ATOMS), f32),
            ],
            in_specs=[vmem] * 6 + [smem] + [vmem] * len(params),
            out_specs=[vmem, vmem],
            scratch_shapes=[pltpu.VMEM(s, d) for s, d in SCRATCH]
            + [pltpu.SemaphoreType.DMA((32,)), pltpu.SemaphoreType.DMA((32,))],
            compiler_params=pltpu.CompilerParams(
                has_side_effects=True, vmem_limit_bytes=60 * 1024 * 1024, **remote
            ),
        )(
            positions,
            species.reshape(1, -1),
            face_rows,
            corner_rows,
            pair_recv,
            pair_send,
            block_count,
            *params,
        )
        return forces, energies.reshape(-1)

    return jax.shard_map(
        per_device,
        mesh=mesh,
        in_specs=(
            P(None, ("gx", "gy")),
            P(("gx", "gy")),
            P(None, ("gx", "gy")),
            P(None, ("gx", "gy")),
            P(("gx", "gy"), None),
            P(("gx", "gy"), None),
            P(("gx", "gy")),
        )
        + (P(),) * 9,
        out_specs=(P(None, ("gx", "gy")), P(("gx", "gy"))),
        check_vma=False,
    )
```

```python
from functools import partial

import jax
import jax.numpy as jnp
from jax import lax
from jax.experimental import pallas as pl
from jax.experimental.pallas import tpu as pltpu
from jax.sharding import PartitionSpec as P

f32 = jnp.float32
bf16 = jnp.bfloat16
i32 = jnp.int32

LAT = 2
C = 128
RH = 64
NB = 8
ATOMS = 256
EXT = 1024
NBLK = 52
PB = 128
PAIRS = NBLK * PB
TM = 1664
T = 512
TILES = PAIRS // T
TB = 1664
SUB = 128
ROWS = 56
STEPS = ((1, 0), (-1, 0), (0, 1), (0, -1), (1, 1), (1, -1), (-1, 1), (-1, -1))
CUTOFF = 2.5
SHARP = 2.0
Q3 = 3.0**0.5
Q5 = 5.0**0.5
Q15 = 15.0**0.5
INV_NEIGH = 0.25
HIGH = lax.Precision.HIGHEST
MESH = pl.DeviceIdType.MESH
L_OF_M = (0, 1, 1, 1, 2, 2, 2, 2, 2)


def dot(a, b):
    return lax.dot_general(a, b, (((1,), (0,)), ((), ())), preferred_element_type=f32)


def dot_nt(a, b):
    return lax.dot_general(a, b, (((1,), (1,)), ((), ())), preferred_element_type=f32)


def dot_exact(a, b):
    return lax.dot_general(
        a, b, (((1,), (0,)), ((), ())), precision=HIGH, preferred_element_type=f32
    )


def parts2(x):
    hi = x.astype(bf16).astype(f32)
    return hi, (x - hi).astype(bf16).astype(f32)


def parts3(x):
    hi = x.astype(bf16).astype(f32)
    rest = x - hi
    mid = rest.astype(bf16).astype(f32)
    return hi, mid, (rest - mid).astype(bf16).astype(f32)


def split2(x):
    hi = x.astype(bf16)
    return hi, (x - hi.astype(f32)).astype(bf16)


def activations(x):
    hi, lo = split2(x)
    return jnp.concatenate([hi, lo, hi, lo], axis=0)


def weights(w):
    hi, lo = parts2(w)
    return jnp.concatenate([hi, hi, lo, lo], axis=0).T.astype(bf16)


def slot_of(k):
    return (128 * k, 128) if k < 4 else (512 + 64 * (k - 4), 64)


def tile_of(k):
    return k if k < 4 else 4 + (k - 4) // 2


def kernel_body(
    sizes,
    pos,
    species,
    face_rows,
    corner_rows,
    pair_recv,
    pair_send,
    block_count,
    embedding,
    radial_in,
    radial_mid,
    radial_out,
    self_weight,
    product_weight,
    readout_linear,
    readout_hidden,
    readout_final,
    forces,
    energies,
    *scratch,
):
    (
        rows6,
        oh6,
        oh6t,
        psrc,
        posout,
        posin,
        ptab,
        geop,
        georow,
        sendrow,
        recvm,
        ohr,
        emb3,
        win4,
        wmid4,
        wout4,
        bmid4,
        bin4,
        bout2,
        bout1,
        z1s,
        z2s,
        rs,
        fg,
        msg_a,
        msg_b,
        acc,
        acc1,
        acc2,
        gacc,
        gbuf_a,
        gbuf_b,
        gf,
        gr,
        gys,
        ge,
        f0t,
        f1t,
        fsend,
        fghost,
        fext,
        gfirst,
        gsend,
        gret,
        gv,
        fs,
        fr,
        gpout,
        gpin,
        send_sem,
        recv_sem,
    ) = scratch
    sums = (acc1, acc2)
    nx, ny = sizes
    alone = nx * ny == 1
    mx = lax.axis_index("gx")
    my = lax.axis_index("gy")

    def neighbour(k, sign):
        dx, dy = STEPS[k]
        return (lax.rem(mx + sign * dx + nx, nx), lax.rem(my + sign * dy + ny, ny))

    if not alone:
        barrier = pltpu.get_barrier_semaphore()
        for k in range(8):
            pl.semaphore_signal(barrier, inc=1, device_id=neighbour(k, 1), device_id_type=MESH)

    def copies(phase, source, target, sign):
        made = []
        for k in range(8):
            if alone:
                made.append(
                    pltpu.make_async_copy(source(k), target(k), recv_sem.at[phase * 8 + k])
                )
            else:
                made.append(
                    pltpu.make_async_remote_copy(
                        src_ref=source(k),
                        dst_ref=target(k),
                        send_sem=send_sem.at[phase * 8 + k],
                        recv_sem=recv_sem.at[phase * 8 + k],
                        device_id=neighbour(k, sign),
                        device_id_type=MESH,
                    )
                )
        return made

    def start(made):
        for c in made:
            c.start()

    def finish(made):
        for c in made:
            c.wait()

    rows6[...] = jnp.zeros_like(rows6)
    rows6[0:4, :] = face_rows[...]
    rows6[4:5, :] = jnp.concatenate([corner_rows[0:1, :], corner_rows[1:2, :]], axis=1)
    rows6[5:6, :] = jnp.concatenate([corner_rows[2:3, :], corner_rows[3:4, :]], axis=1)
    rows_t = rows6[...].astype(f32).T
    atom_sub = lax.broadcasted_iota(i32, (ATOMS, 128), 0)
    atom_lane = lax.broadcasted_iota(i32, (128, ATOMS), 1)
    for h in range(6):
        oh6[:, h * 128 : (h + 1) * 128] = (atom_sub == rows6[h : h + 1, :]).astype(bf16)
        col = jnp.broadcast_to(rows_t[:, h : h + 1], (128, ATOMS)).astype(i32)
        oh6t[h * 128 : (h + 1) * 128, :] = (atom_lane == col).astype(bf16)

    psrc[...] = jnp.zeros_like(psrc)
    psrc[0:3, :] = pos[...]
    psrc[3:4, :] = species[...].astype(f32)
    own = psrc[...]
    three = jnp.concatenate(parts3(own), axis=0).astype(bf16)
    lent = dot(three, oh6[...])
    lent = lent[0:8] + lent[8:16] + lent[16:24]
    for h in range(6):
        posout[h] = lent[:, h * 128 : (h + 1) * 128]
    if not alone:
        pl.semaphore_wait(barrier, 8)
    sent = copies(0, lambda k: posout.at[tile_of(k)], lambda k: posin.at[k], 1)
    start(sent)

    live = lax.broadcasted_iota(i32, (NBLK, PB), 0) < block_count[0]
    recvm[...] = jnp.where(live, pair_recv[...], -1)

    def build(b, carry):
        cols = pl.ds(pl.multiple_of(b * PB, PB), PB)
        send = pair_send[pl.ds(b, 1), :]
        ohr[:, cols] = (atom_sub == recvm[pl.ds(b, 1), :]).astype(bf16)
        sendrow[0:1, cols] = send
        return carry

    lax.fori_loop(0, NBLK, build, 0)

    emb = embedding[...]
    padding = jnp.zeros((6, C), f32)
    pieces = []
    for piece in parts3(emb):
        pieces += [piece, padding]
    pieces.append(jnp.zeros((80, C), f32))
    emb3[...] = jnp.concatenate(pieces, axis=0).T.astype(bf16)

    def prepare(t):
        win = radial_in[t]
        wmid = radial_mid[t]
        wout = radial_out[t]
        win4[...] = weights(win)
        wmid4[...] = weights(wmid)
        wout4[...] = weights(wout)

    def prepare_back(t):
        win = radial_in[t]
        wmid = radial_mid[t]
        wout = radial_out[t]
        bmid4[...] = weights(wmid.T)
        bin4[...] = jnp.concatenate([weights(win.T), jnp.zeros((8, 4 * RH), bf16)], axis=0)
        hi, lo = split2(wout)
        bout2[0:RH, :] = hi
        bout2[RH : 2 * RH, :] = lo
        bout1[...] = hi

    prepare(0)
    species16 = lax.broadcasted_iota(i32, (128, ATOMS), 0) & 15
    f0t[...] = dot(emb3[...], (species16 == species[...]).astype(bf16))

    finish(sent)

    low_half = lax.broadcasted_iota(i32, (8, 128), 1) < 64
    tiles = [own[:, 0:128], own[:, 128:256]]
    shifted = []
    for k in range(8):
        dx, dy = STEPS[k]
        got = posin[k]
        sub = lax.broadcasted_iota(i32, (8, 128), 0)
        shift = jnp.where(sub == 0, f32(dx * LAT), jnp.where(sub == 1, f32(dy * LAT), f32(0)))
        shifted.append(got - shift)
    tiles += shifted[0:4]
    tiles.append(jnp.where(low_half, shifted[4], shifted[5]))
    tiles.append(jnp.where(low_half, shifted[6], shifted[7]))
    for h in range(8):
        ptab[h] = tiles[h]

    send = pair_send[...]
    send_lo = send & 127
    send_hi = lax.shift_right_logical(send, 7)
    recv = pair_recv[...]
    recv_lo = recv & 127
    recv_hi = lax.shift_right_logical(recv, 7)

    def gather(c, lo, hi, count):
        total = jnp.zeros((NBLK, PB), f32)
        for h in range(count):
            row = jnp.broadcast_to(ptab[h][c : c + 1, :], (NBLK, PB))
            total = jnp.where(hi == h, jnp.take_along_axis(row, lo, axis=1), total)
        return total

    vec = [gather(c, send_lo, send_hi, 8) - gather(c, recv_lo, recv_hi, 2) for c in range(3)]
    sender_species = gather(3, send_lo, send_hi, 8)
    square = vec[0] * vec[0] + vec[1] * vec[1] + vec[2] * vec[2]
    square = jnp.where(live, square, 1.0)
    dist = jnp.sqrt(square)
    inv = 1.0 / dist
    ux, uy, uz = [v / dist for v in vec]
    scaled = dist * (1.0 / CUTOFF)
    inside = scaled < 1.0
    room = 1.0 - scaled * scaled
    env = jnp.where(inside, room * room, 0.0)
    denv = jnp.where(inside, (-4.0 / CUTOFF) * scaled * room, 0.0)
    values = [
        dist,
        ux,
        uy,
        uz,
        inv,
        env,
        denv,
        sender_species,
        Q3 * ux,
        Q3 * uy,
        Q3 * uz,
        Q15 * ux * uy,
        Q15 * uy * uz,
        0.5 * Q5 * (3.0 * uz * uz - 1.0),
        Q15 * ux * uz,
        0.5 * Q15 * (ux * ux - uy * uy),
    ]
    for n in range(16):
        geop[n * ROWS : n * ROWS + NBLK, :] = values[n]
    for b in range(NBLK):
        georow[:, b * PB : (b + 1) * PB] = geop[pl.ds(b, 16, stride=ROWS), :]

    def basis_of(geo, width):
        dist = geo[0:1]
        centre = lax.broadcasted_iota(i32, (NB, width), 0).astype(f32) * (CUTOFF / (NB - 1))
        away = dist - centre
        return away, jnp.exp(-SHARP * away * away)

    def radial_pass(i, carry):
        cols = pl.ds(pl.multiple_of(i * TM, TM), TM)
        geo = georow[:, cols]
        away, bump = basis_of(geo, TM)
        hi, lo = parts2(bump * geo[5:6])
        z1 = dot(win4[...], jnp.concatenate([hi, lo, hi, lo], axis=0).astype(bf16))
        z1s[:, cols] = z1
        z2 = dot(wmid4[...], activations(z1 * jax.nn.sigmoid(z1)))
        z2s[:, cols] = z2
        rs[:, cols] = dot(wout4[...], activations(z2 * jax.nn.sigmoid(z2)))
        return carry

    def radial_all():
        lax.fori_loop(0, PAIRS // TM, radial_pass, 0)

    def sender_hot(cols, width):
        rows = lax.broadcasted_iota(jnp.int16, (EXT, width), 0)
        return jnp.where(rows == sendrow[0:1, cols].astype(jnp.int16), bf16(1), bf16(0))

    def first_senders():
        kinds = lax.broadcasted_iota(i32, (128, TM), 0) & 15

        def step(i, carry):
            cols = pl.ds(pl.multiple_of(i * TM, TM), TM)
            fg[:, cols] = dot(emb3[...], (kinds == georow[7:8, cols].astype(i32)).astype(bf16))
            return carry

        lax.fori_loop(0, PAIRS // TM, step, 0)

    def second_senders():
        def step(i, carry):
            cols = pl.ds(pl.multiple_of(i * T, T), T)
            both = dot(fext[...], sender_hot(cols, T))
            fg[:, cols] = both[0:C] + both[C : 2 * C]
            return carry

        lax.fori_loop(0, TILES, step, 0)

    def in_pairs(before, beside):
        before(0, 0)

        def step(j, carry):
            before(2 * j + 1, 1)
            beside(2 * j, 0)
            before(2 * j + 2, 0)
            beside(2 * j + 1, 1)
            return carry

        lax.fori_loop(0, TILES // 2, step, 0)
        beside(TILES - 1, 0)

    def forward(t):
        acc[...] = jnp.zeros_like(acc)
        bufs = (msg_a, msg_b)

        def produce(i, which):
            msg = bufs[which]
            base = pl.multiple_of(i * T, T)
            for s in range(0, T, SUB):
                sub = pl.ds(pl.multiple_of(base + s, SUB), SUB)
                ys = [jnp.broadcast_to(georow[8 + m : 9 + m, sub], (16, SUB)) for m in range(8)]
                for c in range(0, C, 16):
                    f = fg[c : c + 16, sub]
                    p = [rs[l * C + c : l * C + c + 16, sub] * f for l in range(3)]
                    for m in range(9):
                        value = p[0] if m == 0 else p[L_OF_M[m]] * ys[m - 1]
                        hi, lo = split2(value)
                        msg[m * C + c : m * C + c + 16, s : s + SUB] = hi
                        msg[m * C + c : m * C + c + 16, T + s : T + s + SUB] = lo

        def consume(i, which):
            hot = ohr[:, pl.ds(pl.multiple_of(i * T, T), T)]
            acc[...] += dot_nt(bufs[which][...], jnp.concatenate([hot, hot], axis=1))

        in_pairs(produce, consume)
        sums[t][...] = acc[...] * INV_NEIGH

    def invariants(t):
        accn = sums[t]
        a0 = accn[0:C]
        v = accn[C : 2 * C] ** 2
        for m in range(2, 4):
            v = v + accn[m * C : (m + 1) * C] ** 2
        w = accn[4 * C : 5 * C] ** 2
        for m in range(5, 9):
            w = w + accn[m * C : (m + 1) * C] ** 2
        return jnp.concatenate([a0, v, w, a0 * a0], axis=0)

    def node(t, previous):
        return dot_exact(self_weight[t].T, previous) + dot_exact(
            product_weight[t].T, invariants(t)
        )

    def node_back(t, grad):
        accn = sums[t]
        ginv = dot_exact(product_weight[t], grad) * INV_NEIGH
        for m in range(9):
            a = accn[m * C : (m + 1) * C]
            if m == 0:
                g = ginv[0:C] + 2.0 * a * ginv[3 * C : 4 * C]
            else:
                l = L_OF_M[m]
                g = 2.0 * a * ginv[l * C : (l + 1) * C]
            hi, lo = split2(g)
            gacc[m * C : (m + 1) * C, 0:ATOMS] = hi
            gacc[m * C : (m + 1) * C, ATOMS : 2 * ATOMS] = lo

    def backward(first):
        bufs = (gbuf_a, gbuf_b)

        def fetch(i, which):
            hot = ohr[:, pl.ds(pl.multiple_of(i * T, T), T)]
            bufs[which][...] = dot(gacc[...], jnp.concatenate([hot, hot], axis=0))

        def channels(i, which):
            gbuf = bufs[which]
            base = pl.multiple_of(i * T, T)
            for s in range(0, T, SUB):
                sub = pl.ds(pl.multiple_of(base + s, SUB), SUB)
                ys = [jnp.broadcast_to(georow[8 + m : 9 + m, sub], (16, SUB)) for m in range(8)]
                dy = [jnp.zeros((8, SUB), f32) for m in range(8)]
                for c in range(0, C, 16):
                    f = fg[c : c + 16, sub]
                    r = [rs[l * C + c : l * C + c + 16, sub] for l in range(3)]
                    p = [x * f for x in r]
                    tot = [None, None, None]
                    for m in range(9):
                        g = gbuf[m * C + c : m * C + c + 16, s : s + SUB]
                        l = L_OF_M[m]
                        term = g if m == 0 else g * ys[m - 1]
                        tot[l] = term if tot[l] is None else tot[l] + term
                        if m > 0:
                            part = p[l] * g
                            dy[m - 1] = dy[m - 1] + (part[0:8] + part[8:16])
                    if not first:
                        hi, lo = split2(r[0] * tot[0] + r[1] * tot[1] + r[2] * tot[2])
                        gf[c : c + 16, sub] = hi
                        gf[C + c : C + c + 16, sub] = lo
                    for l in range(3):
                        gr[l * C + c : l * C + c + 16, sub] = tot[l] * f
                for m in range(8):
                    gys[m : m + 1, sub] = jnp.sum(dy[m], axis=0, keepdims=True)

        in_pairs(fetch, channels)

        if not first:

            def scatter(i, carry):
                cols = pl.ds(pl.multiple_of(i * T, T), T)
                ge[...] += dot_nt(sender_hot(cols, T), gf[:, cols])
                return carry

            lax.fori_loop(0, TILES, scatter, 0)

        def radial_back(i, carry):
            cols = pl.ds(pl.multiple_of(i * TB, TB), TB)
            hi, lo = split2(gr[:, cols])
            both = dot(bout2[...], hi)
            gh2 = both[0:RH] + both[RH : 2 * RH] + dot(bout1[...], lo)
            z2 = z2s[:, cols]
            sg = jax.nn.sigmoid(z2)
            gh1 = dot(bmid4[...], activations(gh2 * (sg * (1.0 + z2 * (1.0 - sg)))))
            z1 = z1s[:, cols]
            sg = jax.nn.sigmoid(z1)
            gb = dot(bin4[...], activations(gh1 * (sg * (1.0 + z1 * (1.0 - sg)))))[0:NB]
            geo = georow[:, cols]
            gy = [gys[m : m + 1, cols] for m in range(8)]
            away, bump = basis_of(geo, TB)
            slope = bump * (geo[6:7] - (2.0 * SHARP) * away * geo[5:6])
            gdist = jnp.sum(gb * slope, axis=0, keepdims=True)
            ux, uy, uz = geo[1:2], geo[2:3], geo[3:4]
            gux = Q3 * gy[0] + Q15 * (uy * gy[3] + uz * gy[6] + ux * gy[7])
            guy = Q3 * gy[1] + Q15 * (ux * gy[3] + uz * gy[4] - uy * gy[7])
            guz = Q3 * gy[2] + Q15 * (uy * gy[4] + ux * gy[6]) + (3.0 * Q5) * uz * gy[5]
            along = gux * ux + guy * uy + guz * uz
            inv = geo[4:5]
            pull = gdist - inv * along
            out = [pull * ux + inv * gux, pull * uy + inv * guy, pull * uz + inv * guz]
            if not first:
                for n in range(3):
                    gv[n : n + 1, cols] = out[n]
            else:
                out = [out[n] + gv[n : n + 1, cols] for n in range(3)]
                cut = [parts2(x) for x in out]
                zero = jnp.zeros((2, TB), f32)
                base8 = jnp.concatenate([x[0] for x in cut] + [x[1] for x in cut] + [zero], axis=0)
                idx = sendrow[0:1, cols]
                high = lax.shift_right_logical(idx, 7)
                lhs = jnp.concatenate(
                    [jnp.where(high == h, base8, 0.0) for h in range(8)], axis=0
                ).astype(bf16)
                low = (lax.broadcasted_iota(i32, (128, TB), 0) == (idx & 127)).astype(bf16)
                fs[...] += dot_nt(lhs, low)
                lhs = jnp.concatenate([base8, jnp.zeros((8, TB), f32)], axis=0).astype(bf16)
                fr[...] += dot_nt(lhs, ohr[:, cols])
            return carry

        lax.fori_loop(0, PAIRS // TB, radial_back, 0)

    radial_all()
    first_senders()
    forward(0)
    f1t[...] = node(0, f0t[...])

    feat = f1t[...]
    rows = feat.T
    gathered = dot(oh6t[...], jnp.concatenate(parts3(rows), axis=1).astype(bf16))
    fsend[...] = gathered[:, 0:C] + gathered[:, C : 2 * C] + gathered[:, 2 * C : 3 * C]
    sent = copies(
        1, lambda k: fsend.at[pl.ds(*slot_of(k))], lambda k: fghost.at[pl.ds(*slot_of(k))], 1
    )
    start(sent)
    prepare(1)
    prepare_back(1)
    radial_all()
    finish(sent)
    hi, lo = split2(feat)
    fext[0:C, 0:ATOMS] = hi
    fext[C : 2 * C, 0:ATOMS] = lo
    hi, lo = split2(fghost[...].T)
    fext[0:C, ATOMS:EXT] = hi
    fext[C : 2 * C, ATOMS:EXT] = lo

    second_senders()
    forward(1)
    second = node(1, feat)
    hidden = dot_exact(readout_hidden[...].T, second)
    sg = jax.nn.sigmoid(hidden)
    energies[...] = dot_exact(readout_linear[...], feat) + dot_exact(
        readout_final[...], hidden * sg
    )
    weight = readout_final[...].T
    ghidden = weight * (sg * (1.0 + hidden * (1.0 - sg)))
    gsecond = dot_exact(readout_hidden[...], ghidden)
    gfirst[...] = readout_linear[...].T + dot_exact(self_weight[1], gsecond)
    node_back(1, gsecond)
    ge[...] = jnp.zeros_like(ge)
    backward(False)

    gsend[...] = ge[:, 0:C] + ge[:, C : 2 * C]

    def ghost(k):
        offset, size = slot_of(k)
        return gsend.at[pl.ds(ATOMS + offset, size)]

    sent = copies(2, ghost, lambda k: gret.at[pl.ds(*slot_of(k))], -1)
    start(sent)
    prepare(0)
    prepare_back(0)
    radial_all()

    first_senders()
    fs[...] = jnp.zeros_like(fs)
    fr[...] = jnp.zeros_like(fr)
    finish(sent)
    returned = dot(oh6[...], jnp.concatenate(parts3(gret[...]), axis=1).astype(bf16))
    mine = gsend[0:ATOMS, :] + returned[:, 0:C] + returned[:, C : 2 * C] + returned[:, 2 * C :]
    node_back(0, gfirst[...] + mine.T)
    backward(True)

    nothing = jnp.zeros((5, 128), f32)
    tiles = []
    for h in range(8):
        part = fs[8 * h : 8 * h + 8, :]
        tiles.append(jnp.concatenate([part[0:3] + part[3:6], nothing], axis=0))
    for h in range(6):
        gpout[h] = tiles[h + 2]
    sent = copies(3, lambda k: gpout.at[tile_of(k)], lambda k: gpin.at[k], -1)
    start(sent)
    own = jnp.concatenate(tiles[0:2], axis=1)[0:3] - (fr[0:3, :] + fr[3:6, :])
    finish(sent)
    back = [gpin[k] for k in range(4)]
    back.append(jnp.where(low_half, gpin[4], gpin[5]))
    back.append(jnp.where(low_half, gpin[6], gpin[7]))
    three = jnp.concatenate(parts3(jnp.concatenate(back, axis=1)), axis=0).astype(bf16)
    added = dot_nt(three, oh6[...])
    forces[...] = -(own + added[0:3] + added[8:11] + added[16:19])


SCRATCH = (
    ((8, 128), i32),
    ((ATOMS, 768), bf16),
    ((768, ATOMS), bf16),
    ((8, ATOMS), f32),
    ((6, 8, 128), f32),
    ((8, 8, 128), f32),
    ((8, 8, 128), f32),
    ((16 * ROWS, 128), f32),
    ((16, PAIRS), f32),
    ((8, PAIRS), i32),
    ((NBLK, PB), i32),
    ((ATOMS, PAIRS), bf16),
    ((C, 128), bf16),
    ((RH, 4 * NB), bf16),
    ((RH, 4 * RH), bf16),
    ((3 * C, 4 * RH), bf16),
    ((RH, 4 * RH), bf16),
    ((2 * NB, 4 * RH), bf16),
    ((2 * RH, 3 * C), bf16),
    ((RH, 3 * C), bf16),
    ((RH, PAIRS), f32),
    ((RH, PAIRS), f32),
    ((3 * C, PAIRS), f32),
    ((C, PAIRS), f32),
    ((9 * C, 2 * T), bf16),
    ((9 * C, 2 * T), bf16),
    ((9 * C, ATOMS), f32),
    ((9 * C, ATOMS), f32),
    ((9 * C, ATOMS), f32),
    ((9 * C, 2 * ATOMS), bf16),
    ((9 * C, T), f32),
    ((9 * C, T), f32),
    ((2 * C, PAIRS), bf16),
    ((3 * C, PAIRS), f32),
    ((8, PAIRS), f32),
    ((EXT, 2 * C), f32),
    ((C, ATOMS), f32),
    ((C, ATOMS), f32),
    ((768, C), f32),
    ((768, C), f32),
    ((2 * C, EXT), bf16),
    ((C, ATOMS), f32),
    ((EXT, C), f32),
    ((768, C), f32),
    ((8, PAIRS), f32),
    ((64, 128), f32),
    ((16, ATOMS), f32),
    ((6, 8, 128), f32),
    ((8, 8, 128), f32),
)


def solution(mesh):
    sizes = (mesh.shape["gx"], mesh.shape["gy"])

    def per_device(positions, species, face_rows, corner_rows, pair_recv, pair_send, *rest):
        block_count = rest[0]
        params = list(rest[1:])
        params[6] = params[6].reshape(1, -1)
        params[8] = params[8].reshape(1, -1)
        vmem = pl.BlockSpec(memory_space=pltpu.VMEM)
        smem = pl.BlockSpec(memory_space=pltpu.SMEM)
        remote = {"collective_id": 0} if sizes != (1, 1) else {}
        forces, energies = pl.pallas_call(
            partial(kernel_body, sizes),
            out_shape=[
                jax.ShapeDtypeStruct((3, ATOMS), f32),
                jax.ShapeDtypeStruct((1, ATOMS), f32),
            ],
            in_specs=[vmem] * 6 + [smem] + [vmem] * len(params),
            out_specs=[vmem, vmem],
            scratch_shapes=[pltpu.VMEM(s, d) for s, d in SCRATCH]
            + [pltpu.SemaphoreType.DMA((32,)), pltpu.SemaphoreType.DMA((32,))],
            compiler_params=pltpu.CompilerParams(
                has_side_effects=True, vmem_limit_bytes=60 * 1024 * 1024, **remote
            ),
        )(
            positions,
            species.reshape(1, -1),
            face_rows,
            corner_rows,
            pair_recv,
            pair_send,
            block_count,
            *params,
        )
        return forces, energies.reshape(-1)

    return jax.shard_map(
        per_device,
        mesh=mesh,
        in_specs=(
            P(None, ("gx", "gy")),
            P(("gx", "gy")),
            P(None, ("gx", "gy")),
            P(None, ("gx", "gy")),
            P(("gx", "gy"), None),
            P(("gx", "gy"), None),
            P(("gx", "gy")),
        )
        + (P(),) * 9,
        out_specs=(P(None, ("gx", "gy")), P(("gx", "gy"))),
        check_vma=False,
    )
```

```python
from functools import partial

import jax
import jax.numpy as jnp
from jax import lax
from jax.experimental import pallas as pl
from jax.experimental.pallas import tpu as pltpu
from jax.sharding import PartitionSpec as P

f32 = jnp.float32
bf16 = jnp.bfloat16
i32 = jnp.int32

LAT = 2
C = 128
RH = 64
NB = 8
ATOMS = 256
EXT = 1024
NBLK = 52
PB = 128
PAIRS = NBLK * PB
TM = 1664
T = 512
TILES = PAIRS // T
TB = 1664
SUB = 128
ROWS = 56
STEPS = ((1, 0), (-1, 0), (0, 1), (0, -1), (1, 1), (1, -1), (-1, 1), (-1, -1))
CUTOFF = 2.5
SHARP = 2.0
Q3 = 3.0**0.5
Q5 = 5.0**0.5
Q15 = 15.0**0.5
INV_NEIGH = 0.25
HIGH = lax.Precision.HIGHEST
MESH = pl.DeviceIdType.MESH
L_OF_M = (0, 1, 1, 1, 2, 2, 2, 2, 2)


def dot(a, b):
    return lax.dot_general(a, b, (((1,), (0,)), ((), ())), preferred_element_type=f32)


def dot_nt(a, b):
    return lax.dot_general(a, b, (((1,), (1,)), ((), ())), preferred_element_type=f32)


def dot_exact(a, b):
    return lax.dot_general(
        a, b, (((1,), (0,)), ((), ())), precision=HIGH, preferred_element_type=f32
    )


def parts2(x):
    hi = x.astype(bf16).astype(f32)
    return hi, (x - hi).astype(bf16).astype(f32)


def parts3(x):
    hi = x.astype(bf16).astype(f32)
    rest = x - hi
    mid = rest.astype(bf16).astype(f32)
    return hi, mid, (rest - mid).astype(bf16).astype(f32)


def split2(x):
    hi = x.astype(bf16)
    return hi, (x - hi.astype(f32)).astype(bf16)


def activations(x):
    hi, lo = split2(x)
    return jnp.concatenate([hi, lo, hi, lo], axis=0)


def weights(w):
    hi, lo = parts2(w)
    return jnp.concatenate([hi, hi, lo, lo], axis=0).T.astype(bf16)


def slot_of(k):
    return (128 * k, 128) if k < 4 else (512 + 64 * (k - 4), 64)


def tile_of(k):
    return k if k < 4 else 4 + (k - 4) // 2


def kernel_body(
    sizes,
    pos,
    species,
    face_rows,
    corner_rows,
    pair_recv,
    pair_send,
    block_count,
    embedding,
    radial_in,
    radial_mid,
    radial_out,
    self_weight,
    product_weight,
    readout_linear,
    readout_hidden,
    readout_final,
    forces,
    energies,
    *scratch,
):
    (
        rows6,
        oh6,
        oh6t,
        psrc,
        posout,
        posin,
        ptab,
        geop,
        georow,
        sendrow,
        recvm,
        ohr,
        emb3,
        win4,
        wmid4,
        wout4,
        bmid4,
        bin4,
        bout2,
        bout1,
        z1s,
        z2s,
        rs,
        fg,
        msg_a,
        msg_b,
        acc1,
        acc2,
        gacc,
        gbuf_a,
        gbuf_b,
        gf,
        gr,
        gys,
        ge,
        f0t,
        f1t,
        fsend,
        fghost,
        fext,
        gfirst,
        gsend,
        gret,
        gv,
        fs,
        fr,
        gback,
        gvp,
        hot_a,
        hot_b,
        gpout,
        gpin,
        send_sem,
        recv_sem,
    ) = scratch
    sums = (acc1, acc2)
    nx, ny = sizes
    alone = nx * ny == 1
    mx = lax.axis_index("gx")
    my = lax.axis_index("gy")

    def neighbour(k, sign):
        dx, dy = STEPS[k]
        return (lax.rem(mx + sign * dx + nx, nx), lax.rem(my + sign * dy + ny, ny))

    if not alone:
        barrier = pltpu.get_barrier_semaphore()
        for k in range(8):
            pl.semaphore_signal(barrier, inc=1, device_id=neighbour(k, 1), device_id_type=MESH)

    def copies(phase, source, target, sign):
        made = []
        for k in range(8):
            if alone:
                made.append(
                    pltpu.make_async_copy(source(k), target(k), recv_sem.at[phase * 8 + k])
                )
            else:
                made.append(
                    pltpu.make_async_remote_copy(
                        src_ref=source(k),
                        dst_ref=target(k),
                        send_sem=send_sem.at[phase * 8 + k],
                        recv_sem=recv_sem.at[phase * 8 + k],
                        device_id=neighbour(k, sign),
                        device_id_type=MESH,
                    )
                )
        return made

    def start(made):
        for c in made:
            c.start()

    def finish(made):
        for c in made:
            c.wait()

    rows6[...] = jnp.zeros_like(rows6)
    rows6[0:4, :] = face_rows[...]
    rows6[4:5, :] = jnp.concatenate([corner_rows[0:1, :], corner_rows[1:2, :]], axis=1)
    rows6[5:6, :] = jnp.concatenate([corner_rows[2:3, :], corner_rows[3:4, :]], axis=1)
    rows_t = rows6[...].astype(f32).T
    atom_sub = lax.broadcasted_iota(i32, (ATOMS, 128), 0)
    atom_lane = lax.broadcasted_iota(i32, (128, ATOMS), 1)
    for h in range(6):
        oh6[:, h * 128 : (h + 1) * 128] = (atom_sub == rows6[h : h + 1, :]).astype(bf16)
        col = jnp.broadcast_to(rows_t[:, h : h + 1], (128, ATOMS)).astype(i32)
        oh6t[h * 128 : (h + 1) * 128, :] = (atom_lane == col).astype(bf16)

    psrc[...] = jnp.zeros_like(psrc)
    psrc[0:3, :] = pos[...]
    psrc[3:4, :] = species[...].astype(f32)
    own = psrc[...]
    three = jnp.concatenate(parts3(own), axis=0).astype(bf16)
    lent = dot(three, oh6[...])
    lent = lent[0:8] + lent[8:16] + lent[16:24]
    for h in range(6):
        posout[h] = lent[:, h * 128 : (h + 1) * 128]
    if not alone:
        pl.semaphore_wait(barrier, 8)
    sent = copies(0, lambda k: posout.at[tile_of(k)], lambda k: posin.at[k], 1)
    start(sent)

    live = lax.broadcasted_iota(i32, (NBLK, PB), 0) < block_count[0]
    recvm[...] = jnp.where(live, pair_recv[...], -1)

    def build(b, carry):
        cols = pl.ds(pl.multiple_of(b * PB, PB), PB)
        send = pair_send[pl.ds(b, 1), :]
        ohr[:, cols] = (atom_sub == recvm[pl.ds(b, 1), :]).astype(bf16)
        sendrow[0:1, cols] = send
        return carry

    lax.fori_loop(0, NBLK, build, 0)

    emb = embedding[...]
    padding = jnp.zeros((6, C), f32)
    pieces = []
    for piece in parts3(emb):
        pieces += [piece, padding]
    pieces.append(jnp.zeros((80, C), f32))
    emb3[...] = jnp.concatenate(pieces, axis=0).T.astype(bf16)

    def prepare(t):
        win = radial_in[t]
        wmid = radial_mid[t]
        wout = radial_out[t]
        win4[...] = weights(win)
        wmid4[...] = weights(wmid)
        wout4[...] = weights(wout)

    def prepare_back(t):
        win = radial_in[t]
        wmid = radial_mid[t]
        wout = radial_out[t]
        bmid4[...] = weights(wmid.T)
        bin4[...] = jnp.concatenate([weights(win.T), jnp.zeros((8, 4 * RH), bf16)], axis=0)
        hi, lo = split2(wout)
        bout2[0:RH, :] = hi
        bout2[RH : 2 * RH, :] = lo
        bout1[...] = hi

    prepare(0)
    species16 = lax.broadcasted_iota(i32, (128, ATOMS), 0) & 15
    f0t[...] = dot(emb3[...], (species16 == species[...]).astype(bf16))

    finish(sent)

    low_half = lax.broadcasted_iota(i32, (8, 128), 1) < 64
    tiles = [own[:, 0:128], own[:, 128:256]]
    shifted = []
    for k in range(8):
        dx, dy = STEPS[k]
        got = posin[k]
        sub = lax.broadcasted_iota(i32, (8, 128), 0)
        shift = jnp.where(sub == 0, f32(dx * LAT), jnp.where(sub == 1, f32(dy * LAT), f32(0)))
        shifted.append(got - shift)
    tiles += shifted[0:4]
    tiles.append(jnp.where(low_half, shifted[4], shifted[5]))
    tiles.append(jnp.where(low_half, shifted[6], shifted[7]))
    for h in range(8):
        ptab[h] = tiles[h]

    send = pair_send[...]
    send_lo = send & 127
    send_hi = lax.shift_right_logical(send, 7)
    recv = pair_recv[...]
    recv_lo = recv & 127
    recv_hi = lax.shift_right_logical(recv, 7)

    def gather(c, lo, hi, count):
        total = jnp.zeros((NBLK, PB), f32)
        for h in range(count):
            row = jnp.broadcast_to(ptab[h][c : c + 1, :], (NBLK, PB))
            total = jnp.where(hi == h, jnp.take_along_axis(row, lo, axis=1), total)
        return total

    vec = [gather(c, send_lo, send_hi, 8) - gather(c, recv_lo, recv_hi, 2) for c in range(3)]
    sender_species = gather(3, send_lo, send_hi, 8)
    square = vec[0] * vec[0] + vec[1] * vec[1] + vec[2] * vec[2]
    square = jnp.where(live, square, 1.0)
    dist = jnp.sqrt(square)
    inv = 1.0 / dist
    ux, uy, uz = [v / dist for v in vec]
    scaled = dist * (1.0 / CUTOFF)
    inside = scaled < 1.0
    room = 1.0 - scaled * scaled
    env = jnp.where(inside, room * room, 0.0)
    denv = jnp.where(inside, (-4.0 / CUTOFF) * scaled * room, 0.0)
    values = [
        dist,
        ux,
        uy,
        uz,
        inv,
        env,
        denv,
        sender_species,
        Q3 * ux,
        Q3 * uy,
        Q3 * uz,
        Q15 * ux * uy,
        Q15 * uy * uz,
        0.5 * Q5 * (3.0 * uz * uz - 1.0),
        Q15 * ux * uz,
        0.5 * Q15 * (ux * ux - uy * uy),
    ]
    for n in range(16):
        geop[n * ROWS : n * ROWS + NBLK, :] = values[n]
    for b in range(NBLK):
        georow[:, b * PB : (b + 1) * PB] = geop[pl.ds(b, 16, stride=ROWS), :]

    def basis_of(geo, width):
        dist = geo[0:1]
        centre = lax.broadcasted_iota(i32, (NB, width), 0).astype(f32) * (CUTOFF / (NB - 1))
        away = dist - centre
        return away, jnp.exp(-SHARP * away * away)

    def radial_pass(i, carry):
        cols = pl.ds(pl.multiple_of(i * TM, TM), TM)
        geo = georow[:, cols]
        away, bump = basis_of(geo, TM)
        hi, lo = parts2(bump * geo[5:6])
        z1 = dot(win4[...], jnp.concatenate([hi, lo, hi, lo], axis=0).astype(bf16))
        z1s[:, cols] = z1
        z2 = dot(wmid4[...], activations(z1 * jax.nn.sigmoid(z1)))
        z2s[:, cols] = z2
        rs[:, cols] = dot(wout4[...], activations(z2 * jax.nn.sigmoid(z2)))
        return carry

    def radial_all():
        lax.fori_loop(0, PAIRS // TM, radial_pass, 0)

    def sender_hot(cols, width):
        rows = lax.broadcasted_iota(jnp.int16, (EXT, width), 0)
        return jnp.where(rows == sendrow[0:1, cols].astype(jnp.int16), bf16(1), bf16(0))

    def first_senders():
        kinds = lax.broadcasted_iota(i32, (128, TM), 0) & 15

        def step(i, carry):
            cols = pl.ds(pl.multiple_of(i * TM, TM), TM)
            fg[:, cols] = dot(emb3[...], (kinds == georow[7:8, cols].astype(i32)).astype(bf16))
            return carry

        lax.fori_loop(0, PAIRS // TM, step, 0)

    def in_pairs(before, beside):
        before(0, 0)

        def step(j, carry):
            before(2 * j + 1, 1)
            beside(2 * j, 0)
            before(2 * j + 2, 0)
            beside(2 * j + 1, 1)
            return carry

        lax.fori_loop(0, TILES // 2, step, 0)
        beside(TILES - 1, 0)

    hots = (hot_a, hot_b)

    def build_hot(i, which):
        hots[which][...] = sender_hot(pl.ds(pl.multiple_of(i * T, T), T), T)

    def second_senders():
        def step(i, which):
            cols = pl.ds(pl.multiple_of(i * T, T), T)
            both = dot(fext[...], hots[which][...])
            fg[:, cols] = both[0:C] + both[C : 2 * C]

        in_pairs(build_hot, step)

    def forward(t):
        acc = sums[t]
        acc[...] = jnp.zeros_like(acc)
        bufs = (msg_a, msg_b)

        def produce(i, which):
            msg = bufs[which]
            base = pl.multiple_of(i * T, T)
            for s in range(0, T, SUB):
                sub = pl.ds(pl.multiple_of(base + s, SUB), SUB)
                ys = [jnp.broadcast_to(georow[8 + m : 9 + m, sub], (16, SUB)) for m in range(8)]
                for c in range(0, C, 16):
                    f = fg[c : c + 16, sub]
                    p = [rs[l * C + c : l * C + c + 16, sub] * f for l in range(3)]
                    for m in range(9):
                        value = p[0] if m == 0 else p[L_OF_M[m]] * ys[m - 1]
                        hi, lo = split2(value)
                        msg[m * C + c : m * C + c + 16, s : s + SUB] = hi
                        msg[m * C + c : m * C + c + 16, T + s : T + s + SUB] = lo

        def consume(i, which):
            hot = ohr[:, pl.ds(pl.multiple_of(i * T, T), T)]
            acc[...] += dot_nt(bufs[which][...], jnp.concatenate([hot, hot], axis=1))

        in_pairs(produce, consume)
        acc[...] = acc[...] * INV_NEIGH

    def invariants(t):
        accn = sums[t]
        a0 = accn[0:C]
        v = accn[C : 2 * C] ** 2
        for m in range(2, 4):
            v = v + accn[m * C : (m + 1) * C] ** 2
        w = accn[4 * C : 5 * C] ** 2
        for m in range(5, 9):
            w = w + accn[m * C : (m + 1) * C] ** 2
        return jnp.concatenate([a0, v, w, a0 * a0], axis=0)

    def node(t, previous):
        return dot_exact(self_weight[t].T, previous) + dot_exact(
            product_weight[t].T, invariants(t)
        )

    def node_back(t, grad):
        accn = sums[t]
        ginv = dot_exact(product_weight[t], grad) * INV_NEIGH
        for m in range(9):
            a = accn[m * C : (m + 1) * C]
            if m == 0:
                g = ginv[0:C] + 2.0 * a * ginv[3 * C : 4 * C]
            else:
                l = L_OF_M[m]
                g = 2.0 * a * ginv[l * C : (l + 1) * C]
            hi, lo = split2(g)
            gacc[m * C : (m + 1) * C, 0:ATOMS] = hi
            gacc[m * C : (m + 1) * C, ATOMS : 2 * ATOMS] = lo

    def backward(first):
        bufs = (gbuf_a, gbuf_b)

        def fetch(i, which):
            hot = ohr[:, pl.ds(pl.multiple_of(i * T, T), T)]
            bufs[which][...] = dot(gacc[...], jnp.concatenate([hot, hot], axis=0))

        def channels(i, which):
            gbuf = bufs[which]
            base = pl.multiple_of(i * T, T)
            for s in range(0, T, SUB):
                sub = pl.ds(pl.multiple_of(base + s, SUB), SUB)
                ys = [jnp.broadcast_to(georow[8 + m : 9 + m, sub], (16, SUB)) for m in range(8)]
                dy = [jnp.zeros((8, SUB), f32) for m in range(8)]
                for c in range(0, C, 16):
                    f = fg[c : c + 16, sub]
                    r = [rs[l * C + c : l * C + c + 16, sub] for l in range(3)]
                    p = [x * f for x in r]
                    tot = [None, None, None]
                    for m in range(9):
                        g = gbuf[m * C + c : m * C + c + 16, s : s + SUB]
                        l = L_OF_M[m]
                        term = g if m == 0 else g * ys[m - 1]
                        tot[l] = term if tot[l] is None else tot[l] + term
                        if m > 0:
                            part = p[l] * g
                            dy[m - 1] = dy[m - 1] + (part[0:8] + part[8:16])
                    if not first:
                        hi, lo = split2(r[0] * tot[0] + r[1] * tot[1] + r[2] * tot[2])
                        gf[c : c + 16, sub] = hi
                        gf[C + c : C + c + 16, sub] = lo
                    for l in range(3):
                        gr[l * C + c : l * C + c + 16, sub] = tot[l] * f
                for m in range(8):
                    gys[m : m + 1, sub] = jnp.sum(dy[m], axis=0, keepdims=True)

        in_pairs(fetch, channels)

    def scatter_features():
        def step(i, which):
            cols = pl.ds(pl.multiple_of(i * T, T), T)
            ge[...] += dot_nt(hots[which][...], gf[:, cols])

        ge[...] = jnp.zeros_like(ge)
        in_pairs(build_hot, step)

    def backward_radial():
        def radial_back(i, carry):
            cols = pl.ds(pl.multiple_of(i * TB, TB), TB)
            hi, lo = split2(gr[:, cols])
            both = dot(bout2[...], hi)
            gh2 = both[0:RH] + both[RH : 2 * RH] + dot(bout1[...], lo)
            z2 = z2s[:, cols]
            sg = jax.nn.sigmoid(z2)
            gh1 = dot(bmid4[...], activations(gh2 * (sg * (1.0 + z2 * (1.0 - sg)))))
            z1 = z1s[:, cols]
            sg = jax.nn.sigmoid(z1)
            gb = dot(bin4[...], activations(gh1 * (sg * (1.0 + z1 * (1.0 - sg)))))[0:NB]
            geo = georow[:, cols]
            away, bump = basis_of(geo, TB)
            slope = bump * (geo[6:7] - (2.0 * SHARP) * away * geo[5:6])
            gys[8:9, cols] = jnp.sum(gb * slope, axis=0, keepdims=True)
            return carry

        lax.fori_loop(0, PAIRS // TB, radial_back, 0)

    def backward_geometry():
        for b in range(NBLK):
            gback[pl.ds(b, 16, stride=ROWS), :] = gys[:, b * PB : (b + 1) * PB]
        gy = [gback[m * ROWS : m * ROWS + NBLK, :] for m in range(9)]
        ux, uy, uz, inv = [geop[n * ROWS : n * ROWS + NBLK, :] for n in range(1, 5)]
        gux = Q3 * gy[0] + Q15 * (uy * gy[3] + uz * gy[6] + ux * gy[7])
        guy = Q3 * gy[1] + Q15 * (ux * gy[3] + uz * gy[4] - uy * gy[7])
        guz = Q3 * gy[2] + Q15 * (uy * gy[4] + ux * gy[6]) + (3.0 * Q5) * uz * gy[5]
        along = gux * ux + guy * uy + guz * uz
        pull = gy[8] - inv * along
        return [pull * ux + inv * gux, pull * uy + inv * guy, pull * uz + inv * guz]

    def scatter_positions():
        def step(i, carry):
            cols = pl.ds(pl.multiple_of(i * TB, TB), TB)
            base8 = gv[:, cols]
            idx = sendrow[0:1, cols]
            high = lax.shift_right_logical(idx, 7)
            parts = jnp.concatenate(
                [jnp.where(high == h, base8, 0.0) for h in range(8)], axis=0
            ).astype(bf16)
            rows = lax.broadcasted_iota(jnp.int16, (128, TB), 0)
            low = jnp.where(rows == (idx & 127).astype(jnp.int16), bf16(1), bf16(0))
            fs[...] += dot_nt(low, parts)
            whole = jnp.concatenate([base8, jnp.zeros((8, TB), f32)], axis=0).astype(bf16)
            fr[...] += dot_nt(ohr[:, cols], whole)
            return carry

        lax.fori_loop(0, PAIRS // TB, step, 0)

    radial_all()
    gys[8:16, :] = jnp.zeros((8, PAIRS), f32)
    first_senders()
    forward(0)
    f1t[...] = node(0, f0t[...])

    feat = f1t[...]
    rows = feat.T
    gathered = dot(oh6t[...], jnp.concatenate(parts3(rows), axis=1).astype(bf16))
    fsend[...] = gathered[:, 0:C] + gathered[:, C : 2 * C] + gathered[:, 2 * C : 3 * C]
    sent = copies(
        1, lambda k: fsend.at[pl.ds(*slot_of(k))], lambda k: fghost.at[pl.ds(*slot_of(k))], 1
    )
    start(sent)
    prepare(1)
    prepare_back(1)
    radial_all()
    finish(sent)
    hi, lo = split2(feat)
    fext[0:C, 0:ATOMS] = hi
    fext[C : 2 * C, 0:ATOMS] = lo
    hi, lo = split2(fghost[...].T)
    fext[0:C, ATOMS:EXT] = hi
    fext[C : 2 * C, ATOMS:EXT] = lo

    second_senders()
    forward(1)
    second = node(1, feat)
    hidden = dot_exact(readout_hidden[...].T, second)
    sg = jax.nn.sigmoid(hidden)
    energies[...] = dot_exact(readout_linear[...], feat) + dot_exact(
        readout_final[...], hidden * sg
    )
    weight = readout_final[...].T
    ghidden = weight * (sg * (1.0 + hidden * (1.0 - sg)))
    gsecond = dot_exact(readout_hidden[...], ghidden)
    gfirst[...] = readout_linear[...].T + dot_exact(self_weight[1], gsecond)
    node_back(1, gsecond)
    backward(False)
    scatter_features()

    gsend[...] = ge[:, 0:C] + ge[:, C : 2 * C]

    def ghost(k):
        offset, size = slot_of(k)
        return gsend.at[pl.ds(ATOMS + offset, size)]

    sent = copies(2, ghost, lambda k: gret.at[pl.ds(*slot_of(k))], -1)
    start(sent)
    backward_radial()
    out = backward_geometry()
    gvp[...] = jnp.zeros_like(gvp)
    for n in range(3):
        gvp[n * ROWS : n * ROWS + NBLK, :] = out[n]
    prepare(0)
    prepare_back(0)
    radial_all()

    first_senders()
    fs[...] = jnp.zeros_like(fs)
    fr[...] = jnp.zeros_like(fr)
    finish(sent)
    returned = dot(oh6[...], jnp.concatenate(parts3(gret[...]), axis=1).astype(bf16))
    mine = gsend[0:ATOMS, :] + returned[:, 0:C] + returned[:, C : 2 * C] + returned[:, 2 * C :]
    node_back(0, gfirst[...] + mine.T)
    backward(True)
    backward_radial()
    out = backward_geometry()
    for n in range(3):
        hi, lo = parts2(out[n] + gvp[n * ROWS : n * ROWS + NBLK, :])
        gvp[n * ROWS : n * ROWS + NBLK, :] = hi
        gvp[(n + 3) * ROWS : (n + 3) * ROWS + NBLK, :] = lo
    for b in range(NBLK):
        gv[:, b * PB : (b + 1) * PB] = gvp[pl.ds(b, 8, stride=ROWS), :]
    scatter_positions()

    nothing = jnp.zeros((5, 128), f32)
    by_atom = fs[...].T
    by_receiver = fr[...].T
    tiles = []
    for h in range(8):
        part = by_atom[8 * h : 8 * h + 8, :]
        tiles.append(jnp.concatenate([part[0:3] + part[3:6], nothing], axis=0))
    for h in range(6):
        gpout[h] = tiles[h + 2]
    sent = copies(3, lambda k: gpout.at[tile_of(k)], lambda k: gpin.at[k], -1)
    start(sent)
    own = jnp.concatenate(tiles[0:2], axis=1)[0:3] - (by_receiver[0:3] + by_receiver[3:6])
    finish(sent)
    back = [gpin[k] for k in range(4)]
    back.append(jnp.where(low_half, gpin[4], gpin[5]))
    back.append(jnp.where(low_half, gpin[6], gpin[7]))
    three = jnp.concatenate(parts3(jnp.concatenate(back, axis=1)), axis=0).astype(bf16)
    added = dot_nt(three, oh6[...])
    forces[...] = -(own + added[0:3] + added[8:11] + added[16:19])


SCRATCH = (
    ((8, 128), i32),
    ((ATOMS, 768), bf16),
    ((768, ATOMS), bf16),
    ((8, ATOMS), f32),
    ((6, 8, 128), f32),
    ((8, 8, 128), f32),
    ((8, 8, 128), f32),
    ((16 * ROWS, 128), f32),
    ((16, PAIRS), f32),
    ((8, PAIRS), i32),
    ((NBLK, PB), i32),
    ((ATOMS, PAIRS), bf16),
    ((C, 128), bf16),
    ((RH, 4 * NB), bf16),
    ((RH, 4 * RH), bf16),
    ((3 * C, 4 * RH), bf16),
    ((RH, 4 * RH), bf16),
    ((2 * NB, 4 * RH), bf16),
    ((2 * RH, 3 * C), bf16),
    ((RH, 3 * C), bf16),
    ((RH, PAIRS), f32),
    ((RH, PAIRS), f32),
    ((3 * C, PAIRS), f32),
    ((C, PAIRS), f32),
    ((9 * C, 2 * T), bf16),
    ((9 * C, 2 * T), bf16),
    ((9 * C, ATOMS), f32),
    ((9 * C, ATOMS), f32),
    ((9 * C, 2 * ATOMS), bf16),
    ((9 * C, T), f32),
    ((9 * C, T), f32),
    ((2 * C, PAIRS), bf16),
    ((3 * C, PAIRS), f32),
    ((16, PAIRS), f32),
    ((EXT, 2 * C), f32),
    ((C, ATOMS), f32),
    ((C, ATOMS), f32),
    ((768, C), f32),
    ((768, C), f32),
    ((2 * C, EXT), bf16),
    ((C, ATOMS), f32),
    ((EXT, C), f32),
    ((768, C), f32),
    ((8, PAIRS), f32),
    ((128, 64), f32),
    ((ATOMS, 16), f32),
    ((16 * ROWS, 128), f32),
    ((8 * ROWS, 128), f32),
    ((EXT, T), bf16),
    ((EXT, T), bf16),
    ((6, 8, 128), f32),
    ((8, 8, 128), f32),
)


def solution(mesh):
    sizes = (mesh.shape["gx"], mesh.shape["gy"])

    def per_device(positions, species, face_rows, corner_rows, pair_recv, pair_send, *rest):
        block_count = rest[0]
        params = list(rest[1:])
        params[6] = params[6].reshape(1, -1)
        params[8] = params[8].reshape(1, -1)
        vmem = pl.BlockSpec(memory_space=pltpu.VMEM)
        smem = pl.BlockSpec(memory_space=pltpu.SMEM)
        remote = {"collective_id": 0} if sizes != (1, 1) else {}
        forces, energies = pl.pallas_call(
            partial(kernel_body, sizes),
            out_shape=[
                jax.ShapeDtypeStruct((3, ATOMS), f32),
                jax.ShapeDtypeStruct((1, ATOMS), f32),
            ],
            in_specs=[vmem] * 6 + [smem] + [vmem] * len(params),
            out_specs=[vmem, vmem],
            scratch_shapes=[pltpu.VMEM(s, d) for s, d in SCRATCH]
            + [pltpu.SemaphoreType.DMA((32,)), pltpu.SemaphoreType.DMA((32,))],
            compiler_params=pltpu.CompilerParams(
                has_side_effects=True, vmem_limit_bytes=62 * 1024 * 1024, **remote
            ),
        )(
            positions,
            species.reshape(1, -1),
            face_rows,
            corner_rows,
            pair_recv,
            pair_send,
            block_count,
            *params,
        )
        return forces, energies.reshape(-1)

    return jax.shard_map(
        per_device,
        mesh=mesh,
        in_specs=(
            P(None, ("gx", "gy")),
            P(("gx", "gy")),
            P(None, ("gx", "gy")),
            P(None, ("gx", "gy")),
            P(("gx", "gy"), None),
            P(("gx", "gy"), None),
            P(("gx", "gy")),
        )
        + (P(),) * 9,
        out_specs=(P(None, ("gx", "gy")), P(("gx", "gy"))),
        check_vma=False,
    )
```

```python
from functools import partial

import jax
import jax.numpy as jnp
from jax import lax
from jax.experimental import pallas as pl
from jax.experimental.pallas import tpu as pltpu
from jax.sharding import PartitionSpec as P

f32 = jnp.float32
bf16 = jnp.bfloat16
i32 = jnp.int32

LAT = 2
C = 128
RH = 64
NB = 8
ATOMS = 256
EXT = 1024
NBLK = 52
PB = 128
PAIRS = NBLK * PB
TM = 1664
T = 512
TILES = PAIRS // T
TB = 1664
SUB = 128
ROWS = 56
STEPS = ((1, 0), (-1, 0), (0, 1), (0, -1), (1, 1), (1, -1), (-1, 1), (-1, -1))
CUTOFF = 2.5
SHARP = 2.0
Q3 = 3.0**0.5
Q5 = 5.0**0.5
Q15 = 15.0**0.5
INV_NEIGH = 0.25
HIGH = lax.Precision.HIGH
MESH = pl.DeviceIdType.MESH
L_OF_M = (0, 1, 1, 1, 2, 2, 2, 2, 2)


def dot(a, b):
    return lax.dot_general(a, b, (((1,), (0,)), ((), ())), preferred_element_type=f32)


def dot_nt(a, b):
    return lax.dot_general(a, b, (((1,), (1,)), ((), ())), preferred_element_type=f32)


def dot_exact(a, b):
    return lax.dot_general(
        a, b, (((1,), (0,)), ((), ())), precision=HIGH, preferred_element_type=f32
    )


def parts2(x):
    hi = x.astype(bf16).astype(f32)
    return hi, (x - hi).astype(bf16).astype(f32)


def parts3(x):
    hi = x.astype(bf16).astype(f32)
    rest = x - hi
    mid = rest.astype(bf16).astype(f32)
    return hi, mid, (rest - mid).astype(bf16).astype(f32)


def split2(x):
    hi = x.astype(bf16)
    return hi, (x - hi.astype(f32)).astype(bf16)


def activations(x):
    hi, lo = split2(x)
    return jnp.concatenate([hi, lo, hi, lo], axis=0)


def weights(w):
    hi, lo = parts2(w)
    return jnp.concatenate([hi, hi, lo, lo], axis=0).T.astype(bf16)


def slot_of(k):
    return (128 * k, 128) if k < 4 else (512 + 64 * (k - 4), 64)


def tile_of(k):
    return k if k < 4 else 4 + (k - 4) // 2


def kernel_body(
    sizes,
    pos,
    species,
    face_rows,
    corner_rows,
    pair_recv,
    pair_send,
    block_count,
    embedding,
    radial_in,
    radial_mid,
    radial_out,
    self_weight,
    product_weight,
    readout_linear,
    readout_hidden,
    readout_final,
    forces,
    energies,
    *scratch,
):
    (
        rows6,
        oh6,
        oh6t,
        psrc,
        posout,
        posin,
        ptab,
        geop,
        georow,
        sendrow,
        recvm,
        ohr,
        emb3,
        win4,
        wmid4,
        wout4,
        bmid4,
        bin4,
        bout2,
        bout1,
        z1s,
        z2s,
        rs,
        fg,
        msg_a,
        msg_b,
        acc1,
        acc2,
        gacc,
        gbuf_a,
        gbuf_b,
        gf,
        gr,
        gys,
        ge,
        f0t,
        f1t,
        fsend,
        fghost,
        fext,
        gfirst,
        gsend,
        gret,
        gv,
        fs,
        fr,
        gback,
        gvp,
        hot_a,
        hot_b,
        gpout,
        gpin,
        send_sem,
        recv_sem,
    ) = scratch
    sums = (acc1, acc2)
    nx, ny = sizes
    alone = nx * ny == 1
    mx = lax.axis_index("gx")
    my = lax.axis_index("gy")

    def neighbour(k, sign):
        dx, dy = STEPS[k]
        return (lax.rem(mx + sign * dx + nx, nx), lax.rem(my + sign * dy + ny, ny))

    if not alone:
        barrier = pltpu.get_barrier_semaphore()
        for k in range(8):
            pl.semaphore_signal(barrier, inc=1, device_id=neighbour(k, 1), device_id_type=MESH)

    def copies(phase, source, target, sign):
        made = []
        for k in range(8):
            if alone:
                made.append(
                    pltpu.make_async_copy(source(k), target(k), recv_sem.at[phase * 8 + k])
                )
            else:
                made.append(
                    pltpu.make_async_remote_copy(
                        src_ref=source(k),
                        dst_ref=target(k),
                        send_sem=send_sem.at[phase * 8 + k],
                        recv_sem=recv_sem.at[phase * 8 + k],
                        device_id=neighbour(k, sign),
                        device_id_type=MESH,
                    )
                )
        return made

    def start(made):
        for c in made:
            c.start()

    def finish(made):
        for c in made:
            c.wait()

    rows6[...] = jnp.zeros_like(rows6)
    rows6[0:4, :] = face_rows[...]
    rows6[4:5, :] = jnp.concatenate([corner_rows[0:1, :], corner_rows[1:2, :]], axis=1)
    rows6[5:6, :] = jnp.concatenate([corner_rows[2:3, :], corner_rows[3:4, :]], axis=1)
    rows_t = rows6[...].astype(f32).T
    atom_sub = lax.broadcasted_iota(i32, (ATOMS, 128), 0)
    atom_lane = lax.broadcasted_iota(i32, (128, ATOMS), 1)
    for h in range(6):
        oh6[:, h * 128 : (h + 1) * 128] = (atom_sub == rows6[h : h + 1, :]).astype(bf16)

    psrc[...] = jnp.zeros_like(psrc)
    psrc[0:3, :] = pos[...]
    psrc[3:4, :] = species[...].astype(f32)
    own = psrc[...]
    three = jnp.concatenate(parts3(own), axis=0).astype(bf16)
    lent = dot(three, oh6[...])
    lent = lent[0:8] + lent[8:16] + lent[16:24]
    for h in range(6):
        posout[h] = lent[:, h * 128 : (h + 1) * 128]
    if not alone:
        pl.semaphore_wait(barrier, 8)
    sent = copies(0, lambda k: posout.at[tile_of(k)], lambda k: posin.at[k], 1)
    start(sent)

    live = lax.broadcasted_iota(i32, (NBLK, PB), 0) < block_count[0]
    recvm[...] = jnp.where(live, pair_recv[...], -1)
    for h in range(6):
        col = jnp.broadcast_to(rows_t[:, h : h + 1], (128, ATOMS)).astype(i32)
        oh6t[h * 128 : (h + 1) * 128, :] = (atom_lane == col).astype(bf16)

    def build(b, carry):
        cols = pl.ds(pl.multiple_of(b * PB, PB), PB)
        send = pair_send[pl.ds(b, 1), :]
        ohr[:, cols] = (atom_sub == recvm[pl.ds(b, 1), :]).astype(bf16)
        sendrow[0:1, cols] = send
        return carry

    lax.fori_loop(0, NBLK, build, 0)

    emb = embedding[...]
    padding = jnp.zeros((6, C), f32)
    pieces = []
    for piece in parts3(emb):
        pieces += [piece, padding]
    pieces.append(jnp.zeros((80, C), f32))
    emb3[...] = jnp.concatenate(pieces, axis=0).T.astype(bf16)

    def prepare(t):
        win = radial_in[t]
        wmid = radial_mid[t]
        wout = radial_out[t]
        win4[...] = weights(win)
        wmid4[...] = weights(wmid)
        wout4[...] = weights(wout)

    def prepare_back(t):
        win = radial_in[t]
        wmid = radial_mid[t]
        wout = radial_out[t]
        bmid4[...] = weights(wmid.T)
        bin4[...] = jnp.concatenate([weights(win.T), jnp.zeros((8, 4 * RH), bf16)], axis=0)
        hi, lo = split2(wout)
        bout2[0:RH, :] = hi
        bout2[RH : 2 * RH, :] = lo
        bout1[...] = hi

    prepare(0)
    species16 = lax.broadcasted_iota(i32, (128, ATOMS), 0) & 15
    f0t[...] = dot(emb3[...], (species16 == species[...]).astype(bf16))

    finish(sent)

    low_half = lax.broadcasted_iota(i32, (8, 128), 1) < 64
    tiles = [own[:, 0:128], own[:, 128:256]]
    shifted = []
    for k in range(8):
        dx, dy = STEPS[k]
        got = posin[k]
        sub = lax.broadcasted_iota(i32, (8, 128), 0)
        shift = jnp.where(sub == 0, f32(dx * LAT), jnp.where(sub == 1, f32(dy * LAT), f32(0)))
        shifted.append(got - shift)
    tiles += shifted[0:4]
    tiles.append(jnp.where(low_half, shifted[4], shifted[5]))
    tiles.append(jnp.where(low_half, shifted[6], shifted[7]))
    for h in range(8):
        ptab[h] = tiles[h]

    send = pair_send[...]
    send_lo = send & 127
    send_hi = lax.shift_right_logical(send, 7)
    recv = pair_recv[...]
    recv_lo = recv & 127
    recv_hi = lax.shift_right_logical(recv, 7)

    def gather(c, lo, hi, count):
        total = jnp.zeros((NBLK, PB), f32)
        for h in range(count):
            row = jnp.broadcast_to(ptab[h][c : c + 1, :], (NBLK, PB))
            total = jnp.where(hi == h, jnp.take_along_axis(row, lo, axis=1), total)
        return total

    vec = [gather(c, send_lo, send_hi, 8) - gather(c, recv_lo, recv_hi, 2) for c in range(3)]
    sender_species = gather(3, send_lo, send_hi, 8)
    square = vec[0] * vec[0] + vec[1] * vec[1] + vec[2] * vec[2]
    square = jnp.where(live, square, 1.0)
    dist = jnp.sqrt(square)
    inv = 1.0 / dist
    ux, uy, uz = [v / dist for v in vec]
    scaled = dist * (1.0 / CUTOFF)
    inside = scaled < 1.0
    room = 1.0 - scaled * scaled
    env = jnp.where(inside, room * room, 0.0)
    denv = jnp.where(inside, (-4.0 / CUTOFF) * scaled * room, 0.0)
    values = [
        dist,
        ux,
        uy,
        uz,
        inv,
        env,
        denv,
        sender_species,
        Q3 * ux,
        Q3 * uy,
        Q3 * uz,
        Q15 * ux * uy,
        Q15 * uy * uz,
        0.5 * Q5 * (3.0 * uz * uz - 1.0),
        Q15 * ux * uz,
        0.5 * Q15 * (ux * ux - uy * uy),
    ]
    for n in range(16):
        geop[n * ROWS : n * ROWS + NBLK, :] = values[n]
    for b in range(NBLK):
        georow[:, b * PB : (b + 1) * PB] = geop[pl.ds(b, 16, stride=ROWS), :]

    def basis_of(geo, width):
        dist = geo[0:1]
        centre = lax.broadcasted_iota(i32, (NB, width), 0).astype(f32) * (CUTOFF / (NB - 1))
        away = dist - centre
        return away, jnp.exp(-SHARP * away * away)

    def radial_pass(i, carry):
        cols = pl.ds(pl.multiple_of(i * TM, TM), TM)
        geo = georow[:, cols]
        away, bump = basis_of(geo, TM)
        hi, lo = parts2(bump * geo[5:6])
        z1 = dot(win4[...], jnp.concatenate([hi, lo, hi, lo], axis=0).astype(bf16))
        z1s[:, cols] = z1
        z2 = dot(wmid4[...], activations(z1 * jax.nn.sigmoid(z1)))
        z2s[:, cols] = z2
        rs[:, cols] = dot(wout4[...], activations(z2 * jax.nn.sigmoid(z2)))
        return carry

    def radial_all():
        lax.fori_loop(0, PAIRS // TM, radial_pass, 0)

    def sender_hot(cols, width, first, count):
        rows = lax.broadcasted_iota(jnp.int16, (count, width), 0) + jnp.int16(first)
        return jnp.where(rows == sendrow[0:1, cols].astype(jnp.int16), bf16(1), bf16(0))

    def first_senders():
        kinds = lax.broadcasted_iota(i32, (128, TM), 0) & 15

        def step(i, carry):
            cols = pl.ds(pl.multiple_of(i * TM, TM), TM)
            fg[:, cols] = dot(emb3[...], (kinds == georow[7:8, cols].astype(i32)).astype(bf16))
            return carry

        lax.fori_loop(0, PAIRS // TM, step, 0)

    def in_pairs(before, beside):
        def both(later, at_later, now, at_now):
            for q in range(4):
                before(later, at_later, q)
                beside(now, at_now, q)

        for q in range(4):
            before(0, 0, q)

        def step(j, carry):
            both(2 * j + 1, 1, 2 * j, 0)
            both(2 * j + 2, 0, 2 * j + 1, 1)
            return carry

        lax.fori_loop(0, TILES // 2, step, 0)
        for q in range(4):
            beside(TILES - 1, 0, q)

    hots = (hot_a, hot_b)

    def build_hot(i, which, q):
        count = EXT // 4
        cols = pl.ds(pl.multiple_of(i * T, T), T)
        hots[which][q * count : (q + 1) * count, :] = sender_hot(cols, T, q * count, count)

    def second_senders():
        def step(i, which, q):
            if q % 2 == 0:
                half = (q // 2) * (T // 2)
                cols = pl.ds(pl.multiple_of(i * T + half, T // 2), T // 2)
                both = dot(fext[...], hots[which][:, half : half + T // 2])
                fg[:, cols] = both[0:C] + both[C : 2 * C]

        in_pairs(build_hot, step)

    def forward(t):
        acc = sums[t]
        acc[...] = jnp.zeros_like(acc)
        bufs = (msg_a, msg_b)

        def produce(i, which, q):
            msg = bufs[which]
            base = pl.multiple_of(i * T, T)
            for s in (q * SUB,):
                sub = pl.ds(pl.multiple_of(base + s, SUB), SUB)
                ys = [jnp.broadcast_to(georow[8 + m : 9 + m, sub], (16, SUB)) for m in range(8)]
                for c in range(0, C, 16):
                    f = fg[c : c + 16, sub]
                    p = [rs[l * C + c : l * C + c + 16, sub] * f for l in range(3)]
                    for m in range(9):
                        value = p[0] if m == 0 else p[L_OF_M[m]] * ys[m - 1]
                        hi, lo = split2(value)
                        msg[m * C + c : m * C + c + 16, s : s + SUB] = hi
                        msg[m * C + c : m * C + c + 16, T + s : T + s + SUB] = lo

        def consume(i, which, q):
            if q % 2 == 0:
                rows = pl.ds((q // 2) * (9 * C // 2), 9 * C // 2)
                hot = ohr[:, pl.ds(pl.multiple_of(i * T, T), T)]
                acc[rows, :] += dot_nt(bufs[which][rows, :], jnp.concatenate([hot, hot], axis=1))

        in_pairs(produce, consume)
        acc[...] = acc[...] * INV_NEIGH

    def invariants(t):
        accn = sums[t]
        a0 = accn[0:C]
        v = accn[C : 2 * C] ** 2
        for m in range(2, 4):
            v = v + accn[m * C : (m + 1) * C] ** 2
        w = accn[4 * C : 5 * C] ** 2
        for m in range(5, 9):
            w = w + accn[m * C : (m + 1) * C] ** 2
        return jnp.concatenate([a0, v, w, a0 * a0], axis=0)

    def node(t, previous):
        return dot_exact(self_weight[t].T, previous) + dot_exact(
            product_weight[t].T, invariants(t)
        )

    def node_back(t, grad):
        accn = sums[t]
        ginv = dot_exact(product_weight[t], grad) * INV_NEIGH
        for m in range(9):
            a = accn[m * C : (m + 1) * C]
            if m == 0:
                g = ginv[0:C] + 2.0 * a * ginv[3 * C : 4 * C]
            else:
                l = L_OF_M[m]
                g = 2.0 * a * ginv[l * C : (l + 1) * C]
            hi, lo = split2(g)
            gacc[m * C : (m + 1) * C, 0:ATOMS] = hi
            gacc[m * C : (m + 1) * C, ATOMS : 2 * ATOMS] = lo

    def backward(first):
        bufs = (gbuf_a, gbuf_b)

        def fetch(i, which, q):
            if q % 2 == 0:
                half = (q // 2) * (T // 2)
                hot = ohr[:, pl.ds(pl.multiple_of(i * T + half, T // 2), T // 2)]
                bufs[which][:, half : half + T // 2] = dot(
                    gacc[...], jnp.concatenate([hot, hot], axis=0)
                )

        def channels(i, which, q):
            gbuf = bufs[which]
            base = pl.multiple_of(i * T, T)
            for s in (q * SUB,):
                sub = pl.ds(pl.multiple_of(base + s, SUB), SUB)
                ys = [jnp.broadcast_to(georow[8 + m : 9 + m, sub], (16, SUB)) for m in range(8)]
                dy = [jnp.zeros((8, SUB), f32) for m in range(8)]
                for c in range(0, C, 16):
                    f = fg[c : c + 16, sub]
                    r = [rs[l * C + c : l * C + c + 16, sub] for l in range(3)]
                    p = [x * f for x in r]
                    tot = [None, None, None]
                    for m in range(9):
                        g = gbuf[m * C + c : m * C + c + 16, s : s + SUB]
                        l = L_OF_M[m]
                        term = g if m == 0 else g * ys[m - 1]
                        tot[l] = term if tot[l] is None else tot[l] + term
                        if m > 0:
                            part = p[l] * g
                            dy[m - 1] = dy[m - 1] + (part[0:8] + part[8:16])
                    if not first:
                        hi, lo = split2(r[0] * tot[0] + r[1] * tot[1] + r[2] * tot[2])
                        gf[c : c + 16, sub] = hi
                        gf[C + c : C + c + 16, sub] = lo
                    for l in range(3):
                        gr[l * C + c : l * C + c + 16, sub] = tot[l] * f
                for m in range(8):
                    gys[m : m + 1, sub] = jnp.sum(dy[m], axis=0, keepdims=True)

        in_pairs(fetch, channels)

    def scatter_features():
        def step(i, which, q):
            if q % 2 == 0:
                rows = pl.ds((q // 2) * (EXT // 2), EXT // 2)
                cols = pl.ds(pl.multiple_of(i * T, T), T)
                ge[rows, :] += dot_nt(hots[which][rows, :], gf[:, cols])

        ge[...] = jnp.zeros_like(ge)
        in_pairs(build_hot, step)

    def backward_radial():
        def radial_back(i, carry):
            cols = pl.ds(pl.multiple_of(i * TB, TB), TB)
            hi, lo = split2(gr[:, cols])
            both = dot(bout2[...], hi)
            gh2 = both[0:RH] + both[RH : 2 * RH] + dot(bout1[...], lo)
            z2 = z2s[:, cols]
            sg = jax.nn.sigmoid(z2)
            gh1 = dot(bmid4[...], activations(gh2 * (sg * (1.0 + z2 * (1.0 - sg)))))
            z1 = z1s[:, cols]
            sg = jax.nn.sigmoid(z1)
            gb = dot(bin4[...], activations(gh1 * (sg * (1.0 + z1 * (1.0 - sg)))))[0:NB]
            geo = georow[:, cols]
            away, bump = basis_of(geo, TB)
            slope = bump * (geo[6:7] - (2.0 * SHARP) * away * geo[5:6])
            gys[8:9, cols] = jnp.sum(gb * slope, axis=0, keepdims=True)
            return carry

        lax.fori_loop(0, PAIRS // TB, radial_back, 0)

    def backward_geometry():
        for b in range(NBLK):
            gback[pl.ds(b, 16, stride=ROWS), :] = gys[:, b * PB : (b + 1) * PB]
        gy = [gback[m * ROWS : m * ROWS + NBLK, :] for m in range(9)]
        ux, uy, uz, inv = [geop[n * ROWS : n * ROWS + NBLK, :] for n in range(1, 5)]
        gux = Q3 * gy[0] + Q15 * (uy * gy[3] + uz * gy[6] + ux * gy[7])
        guy = Q3 * gy[1] + Q15 * (ux * gy[3] + uz * gy[4] - uy * gy[7])
        guz = Q3 * gy[2] + Q15 * (uy * gy[4] + ux * gy[6]) + (3.0 * Q5) * uz * gy[5]
        along = gux * ux + guy * uy + guz * uz
        pull = gy[8] - inv * along
        return [pull * ux + inv * gux, pull * uy + inv * guy, pull * uz + inv * guz]

    def scatter_positions():
        def step(i, carry):
            cols = pl.ds(pl.multiple_of(i * TB, TB), TB)
            base8 = gv[:, cols]
            idx = sendrow[0:1, cols]
            high = lax.shift_right_logical(idx, 7)
            parts = jnp.concatenate(
                [jnp.where(high == h, base8, 0.0) for h in range(8)], axis=0
            ).astype(bf16)
            rows = lax.broadcasted_iota(jnp.int16, (128, TB), 0)
            low = jnp.where(rows == (idx & 127).astype(jnp.int16), bf16(1), bf16(0))
            fs[...] += dot_nt(low, parts)
            whole = jnp.concatenate([base8, jnp.zeros((8, TB), f32)], axis=0).astype(bf16)
            fr[...] += dot_nt(ohr[:, cols], whole)
            return carry

        lax.fori_loop(0, PAIRS // TB, step, 0)

    radial_all()
    gys[8:16, :] = jnp.zeros((8, PAIRS), f32)
    first_senders()
    forward(0)
    f1t[...] = node(0, f0t[...])

    feat = f1t[...]
    rows = feat.T
    gathered = dot(oh6t[...], jnp.concatenate(parts3(rows), axis=1).astype(bf16))
    fsend[...] = gathered[:, 0:C] + gathered[:, C : 2 * C] + gathered[:, 2 * C : 3 * C]
    sent = copies(
        1, lambda k: fsend.at[pl.ds(*slot_of(k))], lambda k: fghost.at[pl.ds(*slot_of(k))], 1
    )
    start(sent)
    prepare(1)
    prepare_back(1)
    radial_all()
    finish(sent)
    hi, lo = split2(feat)
    fext[0:C, 0:ATOMS] = hi
    fext[C : 2 * C, 0:ATOMS] = lo
    hi, lo = split2(fghost[...].T)
    fext[0:C, ATOMS:EXT] = hi
    fext[C : 2 * C, ATOMS:EXT] = lo

    second_senders()
    forward(1)
    second = node(1, feat)
    hidden = dot_exact(readout_hidden[...].T, second)
    sg = jax.nn.sigmoid(hidden)
    energies[...] = dot_exact(readout_linear[...], feat) + dot_exact(
        readout_final[...], hidden * sg
    )
    weight = readout_final[...].T
    ghidden = weight * (sg * (1.0 + hidden * (1.0 - sg)))
    gsecond = dot_exact(readout_hidden[...], ghidden)
    gfirst[...] = readout_linear[...].T + dot_exact(self_weight[1], gsecond)
    node_back(1, gsecond)
    backward(False)
    scatter_features()

    gsend[...] = ge[:, 0:C] + ge[:, C : 2 * C]

    def ghost(k):
        offset, size = slot_of(k)
        return gsend.at[pl.ds(ATOMS + offset, size)]

    sent = copies(2, ghost, lambda k: gret.at[pl.ds(*slot_of(k))], -1)
    start(sent)
    backward_radial()
    out = backward_geometry()
    gvp[...] = jnp.zeros_like(gvp)
    for n in range(3):
        gvp[n * ROWS : n * ROWS + NBLK, :] = out[n]
    prepare(0)
    prepare_back(0)
    radial_all()

    first_senders()
    fs[...] = jnp.zeros_like(fs)
    fr[...] = jnp.zeros_like(fr)
    finish(sent)
    returned = dot(oh6[...], jnp.concatenate(parts3(gret[...]), axis=1).astype(bf16))
    mine = gsend[0:ATOMS, :] + returned[:, 0:C] + returned[:, C : 2 * C] + returned[:, 2 * C :]
    node_back(0, gfirst[...] + mine.T)
    backward(True)
    backward_radial()
    out = backward_geometry()
    for n in range(3):
        hi, lo = parts2(out[n] + gvp[n * ROWS : n * ROWS + NBLK, :])
        gvp[n * ROWS : n * ROWS + NBLK, :] = hi
        gvp[(n + 3) * ROWS : (n + 3) * ROWS + NBLK, :] = lo
    for b in range(NBLK):
        gv[:, b * PB : (b + 1) * PB] = gvp[pl.ds(b, 8, stride=ROWS), :]
    scatter_positions()

    nothing = jnp.zeros((5, 128), f32)
    by_atom = fs[...].T
    by_receiver = fr[...].T
    tiles = []
    for h in range(8):
        part = by_atom[8 * h : 8 * h + 8, :]
        tiles.append(jnp.concatenate([part[0:3] + part[3:6], nothing], axis=0))
    for h in range(6):
        gpout[h] = tiles[h + 2]
    sent = copies(3, lambda k: gpout.at[tile_of(k)], lambda k: gpin.at[k], -1)
    start(sent)
    own = jnp.concatenate(tiles[0:2], axis=1)[0:3] - (by_receiver[0:3] + by_receiver[3:6])
    finish(sent)
    back = [gpin[k] for k in range(4)]
    back.append(jnp.where(low_half, gpin[4], gpin[5]))
    back.append(jnp.where(low_half, gpin[6], gpin[7]))
    three = jnp.concatenate(parts3(jnp.concatenate(back, axis=1)), axis=0).astype(bf16)
    added = dot_nt(three, oh6[...])
    forces[...] = -(own + added[0:3] + added[8:11] + added[16:19])


SCRATCH = (
    ((8, 128), i32),
    ((ATOMS, 768), bf16),
    ((768, ATOMS), bf16),
    ((8, ATOMS), f32),
    ((6, 8, 128), f32),
    ((8, 8, 128), f32),
    ((8, 8, 128), f32),
    ((16 * ROWS, 128), f32),
    ((16, PAIRS), f32),
    ((8, PAIRS), i32),
    ((NBLK, PB), i32),
    ((ATOMS, PAIRS), bf16),
    ((C, 128), bf16),
    ((RH, 4 * NB), bf16),
    ((RH, 4 * RH), bf16),
    ((3 * C, 4 * RH), bf16),
    ((RH, 4 * RH), bf16),
    ((2 * NB, 4 * RH), bf16),
    ((2 * RH, 3 * C), bf16),
    ((RH, 3 * C), bf16),
    ((RH, PAIRS), f32),
    ((RH, PAIRS), f32),
    ((3 * C, PAIRS), f32),
    ((C, PAIRS), f32),
    ((9 * C, 2 * T), bf16),
    ((9 * C, 2 * T), bf16),
    ((9 * C, ATOMS), f32),
    ((9 * C, ATOMS), f32),
    ((9 * C, 2 * ATOMS), bf16),
    ((9 * C, T), f32),
    ((9 * C, T), f32),
    ((2 * C, PAIRS), bf16),
    ((3 * C, PAIRS), f32),
    ((16, PAIRS), f32),
    ((EXT, 2 * C), f32),
    ((C, ATOMS), f32),
    ((C, ATOMS), f32),
    ((768, C), f32),
    ((768, C), f32),
    ((2 * C, EXT), bf16),
    ((C, ATOMS), f32),
    ((EXT, C), f32),
    ((768, C), f32),
    ((8, PAIRS), f32),
    ((128, 64), f32),
    ((ATOMS, 16), f32),
    ((16 * ROWS, 128), f32),
    ((8 * ROWS, 128), f32),
    ((EXT, T), bf16),
    ((EXT, T), bf16),
    ((6, 8, 128), f32),
    ((8, 8, 128), f32),
)


def solution(mesh):
    sizes = (mesh.shape["gx"], mesh.shape["gy"])

    def per_device(positions, species, face_rows, corner_rows, pair_recv, pair_send, *rest):
        block_count = rest[0]
        params = list(rest[1:])
        params[6] = params[6].reshape(1, -1)
        params[8] = params[8].reshape(1, -1)
        vmem = pl.BlockSpec(memory_space=pltpu.VMEM)
        smem = pl.BlockSpec(memory_space=pltpu.SMEM)
        remote = {"collective_id": 0} if sizes != (1, 1) else {}
        forces, energies = pl.pallas_call(
            partial(kernel_body, sizes),
            out_shape=[
                jax.ShapeDtypeStruct((3, ATOMS), f32),
                jax.ShapeDtypeStruct((1, ATOMS), f32),
            ],
            in_specs=[vmem] * 6 + [smem] + [vmem] * len(params),
            out_specs=[vmem, vmem],
            scratch_shapes=[pltpu.VMEM(s, d) for s, d in SCRATCH]
            + [pltpu.SemaphoreType.DMA((32,)), pltpu.SemaphoreType.DMA((32,))],
            compiler_params=pltpu.CompilerParams(
                has_side_effects=True, vmem_limit_bytes=62 * 1024 * 1024, **remote
            ),
        )(
            positions,
            species.reshape(1, -1),
            face_rows,
            corner_rows,
            pair_recv,
            pair_send,
            block_count,
            *params,
        )
        return forces, energies.reshape(-1)

    return jax.shard_map(
        per_device,
        mesh=mesh,
        in_specs=(
            P(None, ("gx", "gy")),
            P(("gx", "gy")),
            P(None, ("gx", "gy")),
            P(None, ("gx", "gy")),
            P(("gx", "gy"), None),
            P(("gx", "gy"), None),
            P(("gx", "gy")),
        )
        + (P(),) * 9,
        out_specs=(P(None, ("gx", "gy")), P(("gx", "gy"))),
        check_vma=False,
    )
```
